128 devices in a mesh: dev: 128 (over z, x, y, core).
Axes of the slice: x: 4, y: 4, z: 4, core: 2. Of those that a mesh axis runs over, the one named last changes fastest.
Arguments:
- context: bfloat16 [80, 32768], P(None, 'dev'), may hold values from -6 to 6
- depth_logits: bfloat16 [118, 32768], P(None, 'dev'), may hold values from -256 to 256
- send_point: int32 [128, 128, 128], P('dev'), may hold values from -1 to 30207, as said below
- recv_cell: int32 [128, 128, 128], P('dev'), may hold values from -1 to 8191, as said below
- neighbour: int32 [128, 2, 8], P('dev'), may hold values from -1 to 1, as said below
- conv1_weight: bfloat16 [80, 720], replicated, may hold values from -0.21875 to 0.21875
- layer_scale: float32 [80], replicated, may hold values from 32 to 128
- layer_bias: float32 [80], replicated, may hold values from -3 to 3
- conv2_weight: bfloat16 [80, 720], replicated, may hold values from -0.21875 to 0.21875
- out_bias: float32 [80], replicated, may hold values from -3 to 3
Outputs:
- bev_out: float32 [128, 2, 80, 4096], P('dev')
The draws below stay inside these ranges and needn't reach their ends.
Inputs may be any that keep to these rules, and one draw needn't show every extreme that they name: send_point holds -1 or a point of the source device as depth bin times 256 plus pixel; each point stands in at most one slot of its device; in every bucket of 128 slots the used slots come first; some destination receives 128 used slots from every source. recv_cell[t, s, k] is -1 exactly where send_point[s, t, k] is -1, else a cell of tile row t, tile times 4096 plus cell. The neighbour lists come from one grid of tiles in which row t holds 2 active tiles.
All inputs are finite; a program needn't handle non-finite values.
Results may differ from the reference program's by a relative error of at most 0.0045.
Values may be sent and summed in bfloat16 or wider, within the bound.
No kernel may reach another device: no remote copies, remote signals or barrier semaphores. Data moves between devices by JAX's collectives and lax.ppermute only.
A program may use at most 64 MiB of HBM per device.

```python
import math
import jax
import jax.numpy as jnp
from jax import lax

C = 80
DEPTHS = 118
PIX_DEV = 256
CAP = 128
SIDE = 64
TILES_DEV = 2
GRID_COLS = 32
PIXELS = 32768
GRID_ROWS = 128
CELLS = 4096


def routing(key):
    key_heavy, key_forced, key_light, key_points = jax.random.split(key, 4)
    heavy_dest = jax.random.randint(key_heavy, (GRID_ROWS,), 0, 4) == 0
    forced = jax.random.randint(key_forced, (), 0, GRID_ROWS)
    heavy_dest = heavy_dest | (jnp.arange(GRID_ROWS) == forced)
    light_count = jax.random.randint(key_light, (GRID_ROWS, GRID_ROWS), 3 * CAP // 4, CAP + 1)
    counts = jnp.where(heavy_dest[None, :], CAP, light_count)
    filled = jnp.arange(CAP)[None, None, :] < counts[:, :, None]
    point_keys = jax.random.split(key_points, GRID_ROWS)
    points = jax.vmap(lambda one_key: jax.random.permutation(one_key, DEPTHS * PIX_DEV)[:GRID_ROWS * CAP])(point_keys)
    points = points.reshape(GRID_ROWS, GRID_ROWS, CAP).astype(jnp.int32)
    top_point = DEPTHS * PIX_DEV - 1
    first_value = points[:, forced, 0]
    points = jnp.where(points == top_point, first_value[:, None, None], points)
    points = points.at[:, forced, 0].set(top_point)
    return (filled, points.astype(jnp.int32), forced)


def draw_send_point(key, part):
    filled, points, forced = routing(key)
    return jnp.where(filled, points, -1).astype(jnp.int32)


def draw_recv_cell(key, part):
    filled, points, forced = routing(key)
    cell_key = jax.random.fold_in(key, 7)
    cell_pick = jax.random.randint(cell_key, (GRID_ROWS, GRID_ROWS, CAP), 0, TILES_DEV * CELLS)
    cell_pick = cell_pick.at[0, forced, 0].set(TILES_DEV * CELLS - 1)
    return jnp.where(filled, cell_pick, -1).transpose(1, 0, 2).astype(jnp.int32)


def draw_neighbour(key, part):
    key = jax.random.fold_in(key, 11)
    row_keys = jax.random.split(key, GRID_ROWS)
    shuffled = jax.vmap(lambda one_key: jax.random.permutation(one_key, GRID_COLS)[:TILES_DEV])(row_keys)
    columns = jnp.sort(shuffled, axis=1).astype(jnp.int32)
    presence = jnp.any(columns[:, :, None] == jnp.arange(GRID_COLS)[None, None, :], axis=1)
    position = jnp.cumsum(presence.astype(jnp.int32), axis=1) - 1
    lookup = jnp.where(presence, position, -1)
    padded = jnp.pad(lookup, 1, constant_values=-1)
    row_index = jnp.arange(GRID_ROWS)[:, None]
    offsets = [(-1, -1), (-1, 0), (-1, 1), (0, -1), (0, 1), (1, -1), (1, 0), (1, 1)]
    found = [padded[row_index + 1 + offset_row, columns + 1 + offset_col] for offset_row, offset_col in offsets]
    return jnp.stack(found, axis=2).astype(jnp.int32)


def draw_depth_logits(key, part):
    key = jax.random.fold_in(key, 5)
    key_base = jax.random.fold_in(key, 0)
    shape = (DEPTHS, PIXELS)
    return jax.random.normal(key_base, shape, jnp.float32).astype(jnp.bfloat16)


def block_scale(stream_key, shape, shards, least, largest):
    def one(dim, blocks):
        draws = jax.random.uniform(jax.random.fold_in(jax.random.fold_in(stream_key, 6), dim), (blocks,), jnp.float32, least / len(shards), largest / len(shards))
        return jnp.repeat(jnp.exp(draws), shape[dim] // blocks).reshape((-1,) + (1,) * (len(shape) - dim - 1))

    gain = one(*shards[0])
    for cut in shards[1:]:
        gain = gain * one(*cut)
    return gain


def normal_values(rng, shape, spread, most, pieces=(), kind=jnp.bfloat16):
    gain = block_scale(rng, shape, pieces, -0.22, 0.18) if pieces else 1.0
    result = jax.random.normal(rng, shape, jnp.float32) * spread * gain
    return jnp.minimum(jnp.maximum(result, -most), most).astype(kind)


def setup_inputs(seed: int = 0) -> dict:
    key_of = jax.random.split(jax.random.key(seed), 11)
    context = normal_values(key_of[0], (C, PIXELS), 1.0, 6.0, ((1, 128),))
    depth_logits = draw_depth_logits(jax.random.fold_in(key_of[10], 71), 0)
    send_point = draw_send_point(jax.random.fold_in(key_of[10], 71), 0)
    recv_cell = draw_recv_cell(jax.random.fold_in(key_of[10], 71), 0)
    neighbour = draw_neighbour(jax.random.fold_in(key_of[10], 71), 0)
    conv1_weight = normal_values(key_of[5], (C, 9 * C), (9 * C) ** -0.5, 0.21875)
    layer_scale = jnp.clip(jnp.exp(jax.random.uniform(key_of[6], (C,), jnp.float32, math.log(32.0), math.log(128.0))), 32.0, 128.0)
    layer_bias = normal_values(key_of[7], (C,), 0.5, 3.0, (), jnp.float32)
    conv2_weight = normal_values(key_of[8], (C, 9 * C), (9 * C) ** -0.5, 0.21875)
    out_bias = normal_values(key_of[9], (C,), 0.5, 3.0, (), jnp.float32)
    return dict(context=context, depth_logits=depth_logits, send_point=send_point, recv_cell=recv_cell, neighbour=neighbour, conv1_weight=conv1_weight, layer_scale=layer_scale, layer_bias=layer_bias, conv2_weight=conv2_weight, out_bias=out_bias)


def choose(strips, links):
    present = links >= 0
    chosen = jnp.take(strips, jnp.maximum(links, 0), axis=0)
    return chosen * present.astype(chosen.dtype)[:, None, None, None]


def assemble(center, from_above, from_below, links, margin):
    tile_side = center.shape[-1]
    inner = tile_side - margin
    top_band = jnp.concatenate([choose(from_above[..., inner:], links[:, 0]), choose(from_above, links[:, 1]), choose(from_above[..., :margin], links[:, 2])], axis=3)
    middle = jnp.concatenate([choose(center[..., inner:], links[:, 3]), center, choose(center[..., :margin], links[:, 4])], axis=3)
    bottom_band = jnp.concatenate([choose(from_below[..., inner:], links[:, 5]), choose(from_below, links[:, 6]), choose(from_below[..., :margin], links[:, 7])], axis=3)
    return jnp.concatenate([top_band, middle, bottom_band], axis=2)


def conv_tiles(padded, weight):
    channels = padded.shape[1]
    rows_out = padded.shape[2] - 2
    cols_out = padded.shape[3] - 2
    stride = cols_out + 2
    span_length = rows_out * stride
    weight_wide = weight.astype(jnp.float32)

    def one_tile(tile_block):
        flattened = jnp.pad(tile_block.reshape(channels, -1), ((0, 0), (0, 2)))
        stacked = jnp.concatenate([flattened[:, row_shift * stride + column_shift: row_shift * stride + column_shift + span_length] for row_shift in range(3) for column_shift in range(3)], axis=0)
        product = jnp.dot(weight_wide, stacked.astype(jnp.float32), precision=lax.Precision.HIGHEST, preferred_element_type=jnp.float32)
        return product.reshape(-1, rows_out, stride)[:, :, :cols_out]

    return lax.map(one_tile, padded)


def reference(context, depth_logits, send_point, recv_cell, neighbour, conv1_weight, layer_scale, layer_bias, conv2_weight, out_bias):
    depth_prob = jax.nn.softmax(depth_logits.astype(jnp.float32), axis=0).reshape(-1)
    sources = jnp.arange(GRID_ROWS, dtype=jnp.int32)[:, None]
    row_list = jnp.arange(GRID_ROWS, dtype=jnp.int32)

    def splat_row(dest):
        routes = send_point[:, dest, :]
        filled = routes >= 0
        points = jnp.maximum(routes, 0)
        depth_bin = points // PIX_DEV
        pixel_index = sources * PIX_DEV + points % PIX_DEV
        weights = jnp.where(filled, depth_prob[depth_bin * PIXELS + pixel_index], 0.0)
        columns = jnp.take(context, pixel_index.reshape(-1), axis=1).astype(jnp.float32)
        lifted = (columns * weights.reshape(-1)[None, :]).astype(jnp.bfloat16)
        cell_index = recv_cell[dest].reshape(-1)
        target = jnp.where(cell_index >= 0, cell_index, TILES_DEV * CELLS)
        splat_grid = jnp.zeros((C, TILES_DEV * CELLS), jnp.float32).at[:, target].add(lifted.astype(jnp.float32), mode="drop")
        return splat_grid.astype(jnp.bfloat16).reshape(C, TILES_DEV, CELLS).transpose(1, 0, 2)

    bev = lax.map(splat_row, row_list)

    def row_conv(fields, row, weight):
        center = fields[row].reshape(TILES_DEV, C, SIDE, SIDE)
        upper_tiles = fields[jnp.maximum(row - 1, 0)].reshape(TILES_DEV, C, SIDE, SIDE)
        lower_tiles = fields[jnp.minimum(row + 1, GRID_ROWS - 1)].reshape(TILES_DEV, C, SIDE, SIDE)
        from_above = upper_tiles[:, :, SIDE - 1:, :] * (row > 0).astype(fields.dtype)
        from_below = lower_tiles[:, :, :1, :] * (row < GRID_ROWS - 1).astype(fields.dtype)
        padded = assemble(center, from_above, from_below, neighbour[row], 1)
        return conv_tiles(padded, weight)

    def first_layer(row):
        summed = row_conv(bev, row, conv1_weight)
        active = jnp.maximum(layer_scale[None, :, None, None] * summed + layer_bias[None, :, None, None], 0.0)
        return active.astype(jnp.bfloat16).reshape(TILES_DEV, C, CELLS)

    hidden = lax.map(first_layer, row_list)

    def second_layer(row):
        summed = row_conv(hidden, row, conv2_weight)
        return (summed + out_bias[None, :, None, None]).reshape(TILES_DEV, C, CELLS)

    return lax.map(second_layer, row_list)
```

```python
import functools

import jax
import jax.numpy as jnp
from jax import lax
from jax.experimental import pallas as pl
from jax.experimental.pallas import tpu as pltpu
from jax.sharding import PartitionSpec as P

SIDE = 64
CELLS = SIDE * SIDE
BF = jnp.bfloat16
F32 = jnp.float32
VMEM = pl.BlockSpec(memory_space=pltpu.VMEM)
SMEM = pl.BlockSpec(memory_space=pltpu.SMEM)


def params(megabytes):
    return pltpu.CompilerParams(vmem_limit_bytes=megabytes * 1024 * 1024)


def float_iota(shape, axis):
    return lax.broadcasted_iota(jnp.int32, shape, axis).astype(F32).astype(BF)


def lift_kernel(unroll, context, logits, send, out, wide, table):
    channels, pixels = context.shape
    depths = logits.shape[0]
    slots = send.shape[1]
    wide[...] = jnp.full(wide.shape, -1e30, F32)
    wide[0:depths, :] = logits[...].astype(F32)
    shifted = wide[...] - jnp.max(wide[...], axis=0, keepdims=True)
    powers = jnp.exp(shifted)
    prob = powers / jnp.sum(powers, axis=0, keepdims=True)
    high = prob.astype(BF)
    bins = wide.shape[0]
    table[0:channels, :] = context[...]
    table[channels : channels + bins, :] = high
    table[channels + bins : channels + 2 * bins, :] = (prob - high.astype(F32)).astype(BF)
    pixel_iota = float_iota((pixels, slots), 0)
    bin_iota = lax.broadcasted_iota(jnp.int32, (bins, slots), 0)
    one, zero = jnp.ones((), BF), jnp.zeros((), BF)

    def step(i, carry):
        points = [send[pl.ds(i * unroll + u, 1), :] for u in range(unroll)]
        picks = []
        for point in points:
            pixel = (point & (pixels - 1)).astype(F32).astype(BF)
            picks.append(jnp.where(pixel_iota == pixel, one, zero))
        found = jnp.dot(table[...], jnp.concatenate(picks, axis=1), preferred_element_type=F32)
        for u, point in enumerate(points):
            mine = found[:, u * slots : (u + 1) * slots]
            columns = mine[0:channels]
            probs = mine[channels : channels + bins] + mine[channels + bins :]
            chosen = jnp.where(bin_iota == (point >> 8), probs, 0.0)
            weight = jnp.sum(chosen, axis=0, keepdims=True)
            out[i * unroll + u] = (columns * weight).astype(BF)
        return carry

    lax.fori_loop(0, send.shape[0] // unroll, step, 0)


def lift(context, logits, send):
    channels, pixels = context.shape
    return pl.pallas_call(
        functools.partial(lift_kernel, 4),
        out_shape=jax.ShapeDtypeStruct((send.shape[0], channels, send.shape[1]), BF),
        in_specs=[VMEM] * 3,
        out_specs=VMEM,
        scratch_shapes=[pltpu.VMEM((128, pixels), F32), pltpu.VMEM((channels + 256, pixels), BF)],
        compiler_params=params(32),
    )(context, logits, send)


def pack_edges(top0, top1, bottom0, bottom1):
    lower = lax.broadcasted_iota(jnp.int32, top0.shape, 1) < SIDE
    top = jnp.where(lower, top0, pltpu.roll(top1, SIDE, 1))
    bottom = jnp.where(lower, pltpu.roll(bottom1, SIDE, 1), bottom0)
    return top.astype(BF), bottom.astype(BF)


def field_edges(field, tops, bottoms):
    parts = []
    for start in (0, CELLS, CELLS - 128, 2 * CELLS - 128):
        parts.append(field[:, start : start + 128].astype(F32))
    top, bottom = pack_edges(*parts)
    tops[...] = top
    bottoms[...] = bottom


def splat_kernel(groups, unroll, arrived, cells, bev, tops, bottoms, total):
    channels, slots = arrived.shape[1:]
    width = total.shape[1]
    shift = width.bit_length() - 1
    block = 256
    total[...] = jnp.zeros(total.shape, F32)
    cell_iota = float_iota((block, slots * unroll), 0)
    one, zero = jnp.ones((), BF), jnp.zeros((), BF)

    def step(i, carry):
        values = jnp.concatenate([arrived[i * unroll + u] for u in range(unroll)], axis=1)
        targets = jnp.concatenate([cells[pl.ds(i * unroll + u, 1), :] for u in range(unroll)], axis=1)
        group = targets >> shift
        place = targets & (width - 1)
        masked = []
        for g in range(groups):
            masked.append(values * jnp.where(group == g, 1.0, 0.0).astype(BF))
        grouped = jnp.concatenate(masked, axis=0)
        for j in range(width // block):
            spot = (place - j * block).astype(F32).astype(BF)
            pick = jnp.where(cell_iota == spot, one, zero)
            total[:, j * block : (j + 1) * block] += lax.dot_general(
                grouped, pick, (((1,), (1,)), ((), ())), preferred_element_type=F32
            )
        return carry

    lax.fori_loop(0, arrived.shape[0] // unroll, step, 0)
    for g in range(groups):
        bev[:, g * width : (g + 1) * width] = total[g * channels : (g + 1) * channels, :].astype(BF)
    field_edges(bev, tops, bottoms)


def splat(arrived, cells):
    channels = arrived.shape[1]
    groups = 4
    width = 2 * CELLS // groups
    edge = jax.ShapeDtypeStruct((channels, 128), BF)
    return pl.pallas_call(
        functools.partial(splat_kernel, groups, 8),
        out_shape=(jax.ShapeDtypeStruct((channels, 2 * CELLS), BF), edge, edge),
        in_specs=[VMEM] * 2,
        out_specs=(VMEM,) * 3,
        scratch_shapes=[pltpu.VMEM((groups * channels, width), F32)],
        compiler_params=params(32),
    )(arrived, cells)


def halo_images(above, below, links, tile):
    lane = lax.broadcasted_iota(jnp.int32, above.shape, 1)
    lower = lane < SIDE
    column = lane & (SIDE - 1)
    above_other = pltpu.roll(above, SIDE, 1)
    below_other = pltpu.roll(below, SIDE, 1)

    def pick(up, down):
        def gate(n, want):
            return jnp.where(links[tile, n] == want, 1.0, 0.0)

        high = above * gate(up, 0) + above_other * gate(up, 1)
        low = below * gate(down, 0) + below_other * gate(down, 1)
        return jnp.where(lower, low, high)

    west, center, east = pick(0, 5), pick(1, 6), pick(2, 7)
    left = jnp.where(column == 0, pltpu.roll(west, SIDE + 1, 1), pltpu.roll(center, 1, 1))
    right = jnp.where(column == SIDE - 1, pltpu.roll(east, SIDE - 1, 1), pltpu.roll(center, 127, 1))
    return left, center, right


def conv_tile(field, above, below, links, weight, tile, stack, product, finish):
    channels = field.shape[0]
    rows = 16
    shape = (rows, CELLS)
    column = lax.broadcasted_iota(jnp.int32, shape, 1) & (SIDE - 1)
    adjacent = jnp.where(links[tile, 3 if tile else 4] >= 0, 1.0, 0.0)

    def stack_rows(r, carry):
        at = pl.ds(pl.multiple_of(r * rows, rows), rows)
        mine = field[at, tile * CELLS : (tile + 1) * CELLS].astype(F32)
        other = field[at, (1 - tile) * CELLS : (2 - tile) * CELLS].astype(F32) * adjacent
        if tile:
            left_edge, right_edge = pltpu.roll(other, CELLS - SIDE + 1, 1), 0.0
        else:
            left_edge, right_edge = 0.0, pltpu.roll(other, SIDE - 1, 1)
        left = jnp.where(column == 0, left_edge, pltpu.roll(mine, 1, 1))
        right = jnp.where(column == SIDE - 1, right_edge, pltpu.roll(mine, CELLS - 1, 1))
        for b, image in enumerate((left, mine, right)):
            to = pl.ds(pl.multiple_of(b * channels + r * rows, rows), rows)
            stack[to, 0:CELLS] = image.astype(BF)
        return carry

    lax.fori_loop(0, channels // rows, stack_rows, 0)
    images = halo_images(above[...].astype(F32), below[...].astype(F32), links, tile)
    for b, image in enumerate(images):
        stack[b * channels : (b + 1) * channels, CELLS : CELLS + 128] = image.astype(BF)
    span = CELLS + 128
    for start in range(0, span, 512):
        stop = min(start + 512, span)
        product[:, start:stop] = jnp.dot(
            weight[...], stack[:, start:stop], preferred_element_type=F32
        )

    def sum_rows(r, carry):
        def part(a):
            return product[pl.ds(pl.multiple_of(a * channels + r * rows, rows), rows), :]

        below_part = part(2)
        outer = part(0) + jnp.concatenate([below_part[:, 128:], below_part[:, 0:128]], axis=1)
        summed = part(1)[:, 0:CELLS] + pltpu.roll(outer, SIDE, 1)[:, 0:CELLS]
        finish(tile, pl.ds(pl.multiple_of(r * rows, rows), rows), summed)
        return carry

    lax.fori_loop(0, channels // rows, sum_rows, 0)


def first_kernel(field, above, below, links, weight, scale, bias, hidden, tops, bottoms, stack, product):
    def finish(tile, at, summed):
        active = jnp.maximum(scale[at, :] * summed + bias[at, :], 0.0)
        hidden[at, tile * CELLS : (tile + 1) * CELLS] = active.astype(BF)

    for tile in range(2):
        conv_tile(field, above, below, links, weight, tile, stack, product, finish)
    field_edges(hidden, tops, bottoms)


def second_kernel(field, above, below, links, weight, bias, out, stack, product):
    def finish(tile, at, summed):
        out[tile, at, :] = summed + bias[at, :]

    for tile in range(2):
        conv_tile(field, above, below, links, weight, tile, stack, product, finish)


def conv_scratch(channels):
    return [
        pltpu.VMEM((3 * channels, CELLS + 128), BF),
        pltpu.VMEM((3 * channels, CELLS + 128), F32),
    ]


def first_conv(field, above, below, links, weight, scale, bias):
    channels = field.shape[0]
    edge = jax.ShapeDtypeStruct((channels, 128), BF)
    return pl.pallas_call(
        first_kernel,
        out_shape=(jax.ShapeDtypeStruct(field.shape, BF), edge, edge),
        in_specs=[VMEM, VMEM, VMEM, SMEM, VMEM, VMEM, VMEM],
        out_specs=(VMEM,) * 3,
        scratch_shapes=conv_scratch(channels),
        compiler_params=params(32),
    )(field, above, below, links, weight, scale, bias)


def second_conv(field, above, below, links, weight, bias):
    channels = field.shape[0]
    return pl.pallas_call(
        second_kernel,
        out_shape=jax.ShapeDtypeStruct((2, channels, CELLS), F32),
        in_specs=[VMEM, VMEM, VMEM, SMEM, VMEM, VMEM],
        out_specs=VMEM,
        scratch_shapes=conv_scratch(channels),
        compiler_params=params(32),
    )(field, above, below, links, weight, bias)


def exchange(tops, bottoms):
    devices = lax.axis_size("dev")
    above = lax.ppermute(bottoms, "dev", [(i, i + 1) for i in range(devices - 1)])
    below = lax.ppermute(tops, "dev", [(i + 1, i) for i in range(devices - 1)])
    return above, below


def by_row_tap(weight):
    channels = weight.shape[0]
    return weight.reshape(channels, 3, 3 * channels).transpose(1, 0, 2).reshape(3 * channels, -1)


def per_device(
    context,
    depth_logits,
    send_point,
    recv_cell,
    neighbour,
    conv1_weight,
    layer_scale,
    layer_bias,
    conv2_weight,
    out_bias,
):
    lifted = lift(context, depth_logits, send_point[0])
    arrived = lax.all_to_all(lifted, "dev", split_axis=0, concat_axis=0, tiled=True)
    bev, tops, bottoms = splat(arrived, recv_cell[0])
    links = neighbour[0]
    above, below = exchange(tops, bottoms)
    hidden, tops, bottoms = first_conv(
        bev,
        above,
        below,
        links,
        by_row_tap(conv1_weight),
        layer_scale[:, None],
        layer_bias[:, None],
    )
    above, below = exchange(tops, bottoms)
    out = second_conv(hidden, above, below, links, by_row_tap(conv2_weight), out_bias[:, None])
    return out[None]


def solution(mesh):
    in_specs = (
        P(None, "dev"),
        P(None, "dev"),
        P("dev", None, None),
        P("dev", None, None),
        P("dev", None, None),
        P(),
        P(),
        P(),
        P(),
        P(),
    )
    out_specs = P("dev", None, None, None)
    return jax.shard_map(
        per_device, mesh=mesh, in_specs=in_specs, out_specs=out_specs, check_vma=False
    )
```

```python
import functools

import jax
import jax.numpy as jnp
from jax import lax
from jax.experimental import pallas as pl
from jax.experimental.pallas import tpu as pltpu
from jax.sharding import PartitionSpec as P

SIDE = 64
PARTS = (80,)
CELLS = SIDE * SIDE
BF = jnp.bfloat16
F32 = jnp.float32
VMEM = pl.BlockSpec(memory_space=pltpu.VMEM)
SMEM = pl.BlockSpec(memory_space=pltpu.SMEM)


def params(megabytes):
    return pltpu.CompilerParams(vmem_limit_bytes=megabytes * 1024 * 1024)


def float_iota(shape, axis):
    return lax.broadcasted_iota(jnp.int32, shape, axis).astype(F32).astype(BF)


def split_high(value):
    high = value.astype(BF).astype(F32)
    return high, value - high


def lift_kernel(unroll, context, logits, send, *rest):
    *outs, wide, table = rest
    channels, pixels = context.shape
    depths = logits.shape[0]
    slots = send.shape[1]
    bins = -(-depths // 8) * 8
    values = logits[...].astype(F32)
    largest = jnp.max(values, axis=0, keepdims=True)
    inverse = 1.0 / jnp.sum(jnp.exp(values - largest), axis=0, keepdims=True)
    wide[...] = jnp.zeros(wide.shape, F32)
    wide[0:depths, :] = values
    wide[bins : bins + 1, :] = largest
    for n in range(3):
        high, inverse = split_high(inverse)
        wide[bins + 1 + n : bins + 2 + n, :] = high
    table[0:channels, :] = context[...]
    table[channels:, :] = wide[...].astype(BF)
    pixel_iota = float_iota((pixels, slots), 0)
    bin_iota = lax.broadcasted_iota(jnp.int32, (8, slots), 0)
    one, zero = jnp.ones((), BF), jnp.zeros((), BF)

    def step(i, carry):
        points = [send[pl.ds(i * unroll + u, 1), :] for u in range(unroll)]
        picks = []
        for point in points:
            pixel = (point & (pixels - 1)).astype(F32).astype(BF)
            picks.append(jnp.where(pixel_iota == pixel, one, zero))
        for v in range(0, unroll, 2):
            found = jnp.dot(
                table[...], jnp.concatenate(picks[v : v + 2], axis=1), preferred_element_type=F32
            )
            for u in (v, v + 1):
                point = points[u]
                mine = found[:, (u - v) * slots : (u - v + 1) * slots]
                offset = (point >> 8) - bin_iota
                chosen = jnp.zeros((8, slots), F32)
                for r in range(0, bins, 8):
                    chosen = jnp.where(offset == r, mine[channels + r : channels + r + 8], chosen)
                logit = jnp.sum(chosen, axis=0, keepdims=True)
                tail = mine[channels + bins :]
                scale = tail[1:2] + tail[2:3] + tail[3:4]
                weight = jnp.exp(logit - tail[0:1]) * scale
                weight = jnp.where(point >= 0, weight, 0.0)
                lifted = (mine[0:channels] * weight).astype(BF)
                first = 0
                for out in outs:
                    out[i * unroll + u] = lifted[first : first + out.shape[1]]
                    first += out.shape[1]
        return carry

    lax.fori_loop(0, send.shape[0] // unroll, step, 0)


def lift(context, logits, send):
    channels, pixels = context.shape
    return pl.pallas_call(
        functools.partial(lift_kernel, 32),
        out_shape=[jax.ShapeDtypeStruct((send.shape[0], part, send.shape[1]), BF) for part in PARTS],
        in_specs=[VMEM] * 3,
        out_specs=[VMEM] * len(PARTS),
        scratch_shapes=[pltpu.VMEM((128, pixels), F32), pltpu.VMEM((channels + 128, pixels), BF)],
        compiler_params=params(32),
    )(context, logits, send)


def field_edges(field, tops, bottoms):
    for j in range(2):
        at = slice(j * 128, (j + 1) * 128)
        tops[:, at] = field[:, j * CELLS : j * CELLS + 128]
        bottoms[:, at] = field[:, (j + 1) * CELLS - 128 : (j + 1) * CELLS]


def splat_kernel(groups, unroll, arrived, cells, *rest):
    *before, bev = rest[: len(rest) - 1 if len(rest) == 2 else len(rest) - 3]
    total = rest[-1]
    channels, slots = arrived.shape[1:]
    width = total.shape[1]
    shift = width.bit_length() - 1
    block = 256
    total[...] = jnp.zeros(total.shape, F32)
    cell_iota = float_iota((block, slots * unroll), 0)
    one, zero = jnp.ones((), BF), jnp.zeros((), BF)

    def step(i, carry):
        values = jnp.concatenate([arrived[i * unroll + u] for u in range(unroll)], axis=1)
        targets = jnp.concatenate([cells[pl.ds(i * unroll + u, 1), :] for u in range(unroll)], axis=1)
        group = targets >> shift
        place = targets & (width - 1)
        masked = []
        for g in range(groups):
            masked.append(values * jnp.where(group == g, 1.0, 0.0).astype(BF))
        grouped = jnp.concatenate(masked, axis=0)
        for j in range(width // block):
            spot = (place - j * block).astype(F32).astype(BF)
            pick = jnp.where(cell_iota == spot, one, zero)
            total[:, j * block : (j + 1) * block] += lax.dot_general(
                grouped, pick, (((1,), (1,)), ((), ())), preferred_element_type=F32
            )
        return carry

    lax.fori_loop(0, arrived.shape[0] // unroll, step, 0)
    first = bev.shape[0] - channels
    if before:
        bev[0:first, :] = before[0][...]
    for g in range(groups):
        bev[first:, g * width : (g + 1) * width] = total[g * channels : (g + 1) * channels, :].astype(BF)
    if len(rest) > 2:
        field_edges(bev, rest[-3], rest[-2])


def splat(arrived, cells, before=None, last=True):
    channels = arrived.shape[1]
    groups = 4
    while groups * channels < 256:
        groups *= 2
    width = 2 * CELLS // groups
    total = channels + (0 if before is None else before.shape[0])
    edge = jax.ShapeDtypeStruct((total, 256), BF)
    shapes = (jax.ShapeDtypeStruct((total, 2 * CELLS), BF),) + ((edge, edge) if last else ())
    operands = (arrived, cells) + (() if before is None else (before,))
    return pl.pallas_call(
        functools.partial(splat_kernel, groups, 32),
        out_shape=shapes,
        in_specs=[VMEM] * len(operands),
        out_specs=(VMEM,) * len(shapes),
        scratch_shapes=[pltpu.VMEM((groups * channels, width), F32)],
        compiler_params=params(32),
        cost_estimate=pl.CostEstimate(
            flops=2 * arrived.shape[0] * 128 * 2 * CELLS * channels,
            bytes_accessed=arrived.size * 2 + total * 2 * CELLS * 2,
            transcendentals=0,
        ),
    )(*operands)


def lane_images(center, west, east):
    column = lax.broadcasted_iota(jnp.int32, center.shape, 1) & (SIDE - 1)
    left = jnp.where(column == 0, pltpu.roll(west, SIDE + 1, 1), pltpu.roll(center, 1, 1))
    right = jnp.where(column == SIDE - 1, pltpu.roll(east, SIDE - 1, 1), pltpu.roll(center, 127, 1))
    return left, center, right


def halves(low, high):
    return jnp.where(lax.broadcasted_iota(jnp.int32, low.shape, 1) < SIDE, low, high)


def stack_tile(field, links, tile, stack):
    channels = field.shape[0]
    rows = 16
    column = lax.broadcasted_iota(jnp.int32, (rows, CELLS), 1) & (SIDE - 1)
    adjacent = jnp.where(links[tile, 3 if tile else 4] >= 0, 1.0, 0.0)
    for r in range(0, channels, rows):
        mine = field[r : r + rows, tile * CELLS : (tile + 1) * CELLS].astype(F32)
        other = field[r : r + rows, (1 - tile) * CELLS : (2 - tile) * CELLS].astype(F32) * adjacent
        west, east = 0.0, 0.0
        if tile:
            west = pltpu.roll(other, CELLS - SIDE + 1, 1)
        else:
            east = pltpu.roll(other, SIDE - 1, 1)
        left = jnp.where(column == 0, west, pltpu.roll(mine, 1, 1))
        right = jnp.where(column == SIDE - 1, east, pltpu.roll(mine, CELLS - 1, 1))
        stack[r : r + rows, 0:CELLS] = left.astype(BF)
        stack[channels + r : channels + r + rows, 0:CELLS] = field[
            r : r + rows, tile * CELLS : (tile + 1) * CELLS
        ]
        stack[2 * channels + r : 2 * channels + r + rows, 0:CELLS] = right.astype(BF)


def stack_lanes(stack, start, images):
    channels = images[0].shape[0]
    for b, image in enumerate(images):
        stack[b * channels : (b + 1) * channels, start : start + 128] = image.astype(BF)


def multiply(weight, stack, product):
    span = stack.shape[1]
    for start in range(0, span, 512):
        stop = min(start + 512, span)
        product[:, start:stop] = jnp.dot(
            weight[...], stack[:, start:stop], preferred_element_type=F32
        )


def sum_tile(product, finish):
    channels = product.shape[0] // 3
    rows = 16
    for r in range(0, channels, rows):

        def part(a):
            return product[a * channels + r : a * channels + r + rows, :]

        low = part(2)
        outer = part(0) + jnp.concatenate([low[:, 128:], low[:, 0:128]], axis=1)
        finish(r, rows, part(1)[:, 0:CELLS] + pltpu.roll(outer, SIDE, 1)[:, 0:CELLS])


def conv_kernel(
    field,
    above,
    below,
    links,
    weight1,
    weight2,
    scale,
    bias,
    out_bias,
    out,
    stack,
    product,
    side_stack,
    side_product,
    hidden,
    result,
    sems,
):
    channels = field.shape[0]

    def gate(tile, n, want):
        return jnp.where(links[tile, n] == want, 1.0, 0.0)

    def blend(sources, gates):
        return sources[0] * gates[0] + sources[1] * gates[1]

    def halo(low, high, tile):
        def pick(down, up):
            return halves(
                blend(low, [gate(tile, down, k) for k in range(2)]),
                blend(high, [gate(tile, up, k) for k in range(2)]),
            )

        return lane_images(pick(6, 1), pick(5, 0), pick(7, 2))

    def pair(ref):
        return [ref[:, k * 128 : (k + 1) * 128].astype(F32) for k in range(2)]

    upper, lower = pair(above), pair(below)

    for tile in range(2):
        stack_tile(field, links, tile, stack.at[tile])
        stack_lanes(stack.at[tile], CELLS, halo(lower, upper, tile))
        multiply(weight1, stack.at[tile], product.at[tile])

        def finish(r, rows, summed):
            active = jnp.maximum(scale[r : r + rows, :] * summed + bias[r : r + rows, :], 0.0)
            hidden[r : r + rows, tile * CELLS : (tile + 1) * CELLS] = active.astype(BF)

        sum_tile(product.at[tile], finish)

    first = [field[:, j * CELLS : j * CELLS + 128].astype(F32) for j in range(2)]
    last = [field[:, (j + 1) * CELLS - 128 : (j + 1) * CELLS].astype(F32) for j in range(2)]

    def joined(west, center, east):
        found = 0.0
        for j in range(2):
            for a, b in ((west, center), (center, east)):
                found = jnp.maximum(found, gate(j, a, 0) * gate(j, b, 1))
        return found

    joined_up, joined_down = joined(0, 1, 2), joined(5, 6, 7)
    for k in range(2):
        for start, source, flag in ((0, upper, joined_up), (256, lower, joined_down)):
            other = source[1 - k] * flag
            none = jnp.zeros_like(other)
            images = lane_images(source[k], other if k else none, none if k else other)
            stack_lanes(side_stack, start + k * 128, images)

        def own(up, down):
            return halves(
                blend(first, [gate(j, up, k) for j in range(2)]),
                blend(last, [gate(j, down, k) for j in range(2)]),
            )

        stack_lanes(side_stack, 512 + k * 128, lane_images(own(1, 6), own(2, 7), own(0, 5)))
    multiply(weight1, side_stack, side_product)
    sides = []
    for k in range(2):

        def part(a, kind):
            start = kind * 256 + k * 128
            return side_product[a * channels : (a + 1) * channels, start : start + 128]

        down_row = part(1, 1) + pltpu.roll(part(2, 1) + part(0, 2), SIDE, 1)
        up_row = part(1, 0) + pltpu.roll(part(0, 0) + part(2, 2), SIDE, 1)
        summed = halves(down_row, up_row)
        active = jnp.maximum(scale[...] * summed + bias[...], 0.0)
        sides.append(active.astype(BF).astype(F32))

    copies = []
    for tile in range(2):
        stack_tile(hidden, links, tile, stack.at[tile])
        stack_lanes(stack.at[tile], CELLS, halo(sides, sides, tile))
        multiply(weight2, stack.at[tile], product.at[tile])

        def finish(r, rows, summed):
            result[tile, r : r + rows, :] = summed + out_bias[r : r + rows, :]
            copy = pltpu.make_async_copy(
                result.at[tile, r : r + rows],
                out.at[tile, r : r + rows],
                sems.at[tile, r // rows],
            )
            copy.start()
            copies.append(copy)

        sum_tile(product.at[tile], finish)
    for copy in copies:
        copy.wait()


def convolutions(field, above, below, links, weight1, weight2, scale, bias, out_bias):
    channels = field.shape[0]
    span = CELLS + 128
    return pl.pallas_call(
        conv_kernel,
        out_shape=jax.ShapeDtypeStruct((2, channels, CELLS), F32),
        in_specs=[VMEM, VMEM, VMEM, SMEM] + [VMEM] * 5,
        out_specs=pl.BlockSpec(memory_space=pl.ANY),
        scratch_shapes=[
            pltpu.VMEM((2, 3 * channels, span), BF),
            pltpu.VMEM((2, 3 * channels, span), F32),
            pltpu.VMEM((3 * channels, 768), BF),
            pltpu.VMEM((3 * channels, 768), F32),
            pltpu.VMEM((channels, 2 * CELLS), BF),
            pltpu.VMEM((2, channels, CELLS), F32),
            pltpu.SemaphoreType.DMA((2, channels // 16)),
        ],
        compiler_params=params(40),
    )(field, above, below, links, weight1, weight2, scale, bias, out_bias)


def exchange(tops, bottoms):
    devices = lax.axis_size("dev")
    above = lax.ppermute(bottoms, "dev", [(i, i + 1) for i in range(devices - 1)])
    below = lax.ppermute(tops, "dev", [(i + 1, i) for i in range(devices - 1)])
    return above, below


def by_row_tap(weight):
    channels = weight.shape[0]
    return weight.reshape(channels, 3, 3 * channels).transpose(1, 0, 2).reshape(3 * channels, -1)


def per_device(
    context,
    depth_logits,
    send_point,
    recv_cell,
    neighbour,
    conv1_weight,
    layer_scale,
    layer_bias,
    conv2_weight,
    out_bias,
):
    lifted = lift(context, depth_logits, send_point[0])
    arrived = [
        lax.all_to_all(part, "dev", split_axis=0, concat_axis=0, tiled=True) for part in lifted
    ]
    bev, tops, bottoms = splat(arrived[0], recv_cell[0])
    above, below = exchange(tops, bottoms)
    out = convolutions(
        bev,
        above,
        below,
        neighbour[0],
        by_row_tap(conv1_weight),
        by_row_tap(conv2_weight),
        layer_scale[:, None],
        layer_bias[:, None],
        out_bias[:, None],
    )
    return out[None]


def solution(mesh):
    in_specs = (
        P(None, "dev"),
        P(None, "dev"),
        P("dev", None, None),
        P("dev", None, None),
        P("dev", None, None),
        P(),
        P(),
        P(),
        P(),
        P(),
    )
    out_specs = P("dev", None, None, None)
    return jax.shard_map(
        per_device, mesh=mesh, in_specs=in_specs, out_specs=out_specs, check_vma=False
    )
```

```python
import functools

import jax
import jax.numpy as jnp
from jax import lax
from jax.experimental import pallas as pl
from jax.experimental.pallas import tpu as pltpu
from jax.sharding import PartitionSpec as P

SIDE = 64
CELLS = SIDE * SIDE
BF = jnp.bfloat16
F32 = jnp.float32
VMEM = pl.BlockSpec(memory_space=pltpu.VMEM)
SMEM = pl.BlockSpec(memory_space=pltpu.SMEM)


def params(megabytes):
    return pltpu.CompilerParams(vmem_limit_bytes=megabytes * 1024 * 1024)


def float_iota(shape, axis):
    return lax.broadcasted_iota(jnp.int32, shape, axis).astype(F32).astype(BF)


def split_high(value):
    high = value.astype(BF).astype(F32)
    return high, value - high


def lift_kernel(unroll, context_in, logits_in, send_in, out, lifted, context, logits, send, wide, table, sems):
    pairs = ((logits_in, logits), (context_in, context), (send_in, send))
    copies = [pltpu.make_async_copy(a, b, sems.at[n]) for n, (a, b) in enumerate(pairs)]
    for copy in copies:
        copy.start()
    channels, pixels = context.shape
    depths = logits.shape[0]
    slots = send.shape[1]
    bins = -(-depths // 8) * 8
    copies[0].wait()
    values = logits[...].astype(F32)
    largest = jnp.max(values, axis=0, keepdims=True)
    inverse = 1.0 / jnp.sum(jnp.exp(values - largest), axis=0, keepdims=True)
    wide[...] = jnp.zeros(wide.shape, F32)
    wide[0:depths, :] = values
    wide[bins : bins + 1, :] = largest
    for n in range(3):
        high, inverse = split_high(inverse)
        wide[bins + 1 + n : bins + 2 + n, :] = high
    copies[1].wait()
    copies[2].wait()
    table[0:channels, :] = context[...]
    table[channels:, :] = wide[...].astype(BF)
    pixel_iota = float_iota((pixels, slots), 0)
    bin_iota = lax.broadcasted_iota(jnp.int32, (8, slots), 0)
    one, zero = jnp.ones((), BF), jnp.zeros((), BF)

    def step(i, carry):
        points = [send[pl.ds(i * unroll + u, 1), :] for u in range(unroll)]
        picks = []
        for point in points:
            pixel = (point & (pixels - 1)).astype(F32).astype(BF)
            picks.append(jnp.where(pixel_iota == pixel, one, zero))
        for v in range(0, unroll, 2):
            found = jnp.dot(
                table[...], jnp.concatenate(picks[v : v + 2], axis=1), preferred_element_type=F32
            )
            for u in (v, v + 1):
                point = points[u]
                mine = found[:, (u - v) * slots : (u - v + 1) * slots]
                offset = (point >> 8) - bin_iota
                chosen = jnp.zeros((8, slots), F32)
                for r in range(0, bins, 8):
                    chosen = jnp.where(offset == r, mine[channels + r : channels + r + 8], chosen)
                logit = jnp.sum(chosen, axis=0, keepdims=True)
                tail = mine[channels + bins :]
                scale = tail[1:2] + tail[2:3] + tail[3:4]
                weight = jnp.exp(logit - tail[0:1]) * scale
                weight = jnp.where(point >= 0, weight, 0.0)
                lifted[i * unroll + u] = (mine[0:channels] * weight).astype(BF)
        leave(i).start()
        return carry

    def leave(i):
        at = pl.ds(i * unroll, unroll)
        return pltpu.make_async_copy(lifted.at[at], out.at[at], sems.at[3 + i])

    lax.fori_loop(0, send.shape[0] // unroll, step, 0)
    for i in range(send.shape[0] // unroll):
        leave(i).wait()


def lift(context, logits, send):
    channels, pixels = context.shape
    return pl.pallas_call(
        functools.partial(lift_kernel, 32),
        out_shape=jax.ShapeDtypeStruct((send.shape[0], channels, send.shape[1]), BF),
        in_specs=[pl.BlockSpec(memory_space=pl.ANY)] * 3,
        out_specs=pl.BlockSpec(memory_space=pl.ANY),
        scratch_shapes=[
            pltpu.VMEM((send.shape[0], channels, send.shape[1]), BF),
            pltpu.VMEM(context.shape, BF),
            pltpu.VMEM(logits.shape, BF),
            pltpu.VMEM(send.shape, jnp.int32),
            pltpu.VMEM((128, pixels), F32),
            pltpu.VMEM((channels + 128, pixels), BF),
            pltpu.SemaphoreType.DMA((3 + send.shape[0] // 32,)),
        ],
        compiler_params=params(60),
    )(context, logits, send)


def field_edges(field, tops, bottoms):
    tops[...] = field[:, 0:256]
    bottoms[...] = field[:, 2 * CELLS - 256 : 2 * CELLS]


def splat_kernel(groups, unroll, arrived, cells, *rest):
    *before, bev = rest[: len(rest) - 1 if len(rest) == 2 else len(rest) - 3]
    total = rest[-1]
    channels, slots = arrived.shape[1:]
    width = total.shape[1]
    shift = width.bit_length() - 1
    block = 256
    total[...] = jnp.zeros(total.shape, F32)
    cell_iota = float_iota((block, slots * unroll), 0)
    one, zero = jnp.ones((), BF), jnp.zeros((), BF)

    def step(i, carry):
        values = jnp.concatenate([arrived[i * unroll + u] for u in range(unroll)], axis=1)
        targets = jnp.concatenate([cells[pl.ds(i * unroll + u, 1), :] for u in range(unroll)], axis=1)
        row, x = (targets >> 6) & (SIDE - 1), targets & (SIDE - 1)
        targets = jnp.where(targets < 0, -1, row * 128 + (targets >> 12) * SIDE + x)
        group = targets >> shift
        place = targets & (width - 1)
        masked = []
        for g in range(groups):
            masked.append(values * jnp.where(group == g, 1.0, 0.0).astype(BF))
        grouped = jnp.concatenate(masked, axis=0)
        for j in range(width // block):
            spot = (place - j * block).astype(F32).astype(BF)
            pick = jnp.where(cell_iota == spot, one, zero)
            total[:, j * block : (j + 1) * block] += lax.dot_general(
                grouped, pick, (((1,), (1,)), ((), ())), preferred_element_type=F32
            )
        return carry

    lax.fori_loop(0, arrived.shape[0] // unroll, step, 0)
    first = bev.shape[0] - channels
    if before:
        bev[0:first, :] = before[0][...]
    for g in range(groups):
        bev[first:, g * width : (g + 1) * width] = total[g * channels : (g + 1) * channels, :].astype(BF)
    if len(rest) > 2:
        field_edges(bev, rest[-3], rest[-2])


def splat(arrived, cells, before=None, last=True):
    channels = arrived.shape[1]
    groups = 4
    while groups * channels < 256:
        groups *= 2
    width = 2 * CELLS // groups
    total = channels + (0 if before is None else before.shape[0])
    edge = jax.ShapeDtypeStruct((total, 256), BF)
    shapes = (jax.ShapeDtypeStruct((total, 2 * CELLS), BF),) + ((edge, edge) if last else ())
    operands = (arrived, cells) + (() if before is None else (before,))
    return pl.pallas_call(
        functools.partial(splat_kernel, groups, 32),
        out_shape=shapes,
        in_specs=[VMEM] * len(operands),
        out_specs=(VMEM,) * len(shapes),
        scratch_shapes=[pltpu.VMEM((groups * channels, width), F32)],
        compiler_params=params(32),
        cost_estimate=pl.CostEstimate(
            flops=2 * arrived.shape[0] * 128 * 2 * CELLS * channels,
            bytes_accessed=arrived.size * 2 + total * 2 * CELLS * 2,
            transcendentals=0,
        ),
    )(*operands)


def conv_kernel(
    field,
    above,
    below,
    links,
    weight1,
    weight2,
    scale,
    bias,
    out_bias,
    out,
    stack1,
    stack2,
    side_stack,
    result,
    sems,
):
    channels = field.shape[0]
    shape = (channels, 128)
    lane = lax.broadcasted_iota(jnp.int32, shape, 1)
    lower = lane < SIDE
    column = lane & (SIDE - 1)

    def gate(tile, n, want):
        return jnp.where(links[tile, n] == want, 1.0, 0.0)

    def block(ref, y):
        return ref[:, y * 128 : (y + 1) * 128]

    def put(stack, slot, left, center, right):
        for b, image in enumerate((left, center, right)):
            stack[b * channels : (b + 1) * channels, slot * 128 : (slot + 1) * 128] = image.astype(BF)

    def keeps(joined):
        left = jnp.where(lane == 0, 0.0, jnp.where(lane == SIDE, joined, 1.0))
        right = jnp.where(lane == 127, 0.0, jnp.where(lane == SIDE - 1, joined, 1.0))
        return left, right

    def put_row(stack, slot, row, keep):
        wide = row.astype(F32)
        put(stack, slot, pltpu.roll(wide, 1, 1) * keep[0], row, pltpu.roll(wide, 127, 1) * keep[1])

    def put_mapped(stack, slot, source, west, center, east, inverse=False):
        swapped = pltpu.roll(source, SIDE, 1)

        def mapped(n):
            cross = [gate(0, n, 1), gate(1, n, 0)]
            if inverse:
                cross.reverse()
            same = jnp.where(lower, gate(0, n, 0), gate(1, n, 1))
            return source * same + swapped * jnp.where(lower, cross[0], cross[1])

        middle = mapped(center)
        left = jnp.where(column == 0, pltpu.roll(mapped(west), SIDE + 1, 1), pltpu.roll(middle, 1, 1))
        right = jnp.where(
            column == SIDE - 1, pltpu.roll(mapped(east), SIDE - 1, 1), pltpu.roll(middle, 127, 1)
        )
        put(stack, slot, left, middle, right)

    def multiply(weight, stack, product, start, stop):
        found = jnp.dot(
            weight[...], stack[:, start * 128 : stop * 128], preferred_element_type=F32
        )
        for slot in range(start, stop):
            lanes = slice((slot - start) * 128, (slot - start + 1) * 128)
            for a in range(3):
                product[a, slot] = found[a * channels : (a + 1) * channels, lanes]

    def summed(product, slots):
        first, second, third = (product.pop((a, slot)) for a, slot in enumerate(slots))
        return first + second + third

    def joined(west, center, east):
        found = 0.0
        for j in range(2):
            for a, b in ((west, center), (center, east)):
                found = jnp.maximum(found, gate(j, a, 0) * gate(j, b, 1))
        return found

    gain = jnp.broadcast_to(scale[...], shape)
    shift = jnp.broadcast_to(bias[...], shape)
    last_shift = jnp.broadcast_to(out_bias[...], shape)
    keep = keeps(gate(1, 3, 0))
    keep_up, keep_down = keeps(joined(0, 1, 2)), keeps(joined(5, 6, 7))
    end = SIDE + 1
    product1, product2, side_product = {}, {}, {}

    def activate(value):
        return jnp.maximum(gain * value + shift, 0.0).astype(BF)

    put_row(side_stack, 0, block(above, 0), keep_up)
    put_row(side_stack, 1, block(above, 1), keep_up)
    put_mapped(side_stack, 2, block(field, 0).astype(F32), 2, 1, 0, True)
    put_mapped(side_stack, 3, block(field, SIDE - 1).astype(F32), 7, 6, 5, True)
    put_row(side_stack, 4, block(below, 0), keep_down)
    put_row(side_stack, 5, block(below, 1), keep_down)
    multiply(weight1, side_stack, side_product, 0, 6)
    up_row = activate(summed(side_product, (0, 1, 2))).astype(F32)
    down_row = activate(summed(side_product, (3, 4, 5))).astype(F32)
    put_mapped(stack2, 0, up_row, 0, 1, 2)
    put_mapped(stack2, end, down_row, 5, 6, 7)
    put_mapped(stack1, 0, block(above, 1).astype(F32), 0, 1, 2)
    put_mapped(stack1, end, block(below, 0).astype(F32), 5, 6, 7)

    step = 16
    done = 0
    for start in range(0, SIDE + 2, step):
        stop = min(start + step, SIDE + 2)
        for slot in range(max(start, 1), min(stop, end)):
            put_row(stack1, slot, block(field, slot - 1), keep)
        multiply(weight1, stack1, product1, start, stop)
        while done < stop - 2:
            put_row(stack2, done + 1, activate(summed(product1, (done, done + 1, done + 2))), keep)
            done += 1

    copies = []
    done = 0
    part = 16
    for start in range(0, SIDE + 2, step):
        stop = min(start + step, SIDE + 2)
        multiply(weight2, stack2, product2, start, stop)
        while done + 1 < stop - 2:
            even = summed(product2, (done, done + 1, done + 2)) + last_shift
            odd = summed(product2, (done + 1, done + 2, done + 3)) + last_shift
            at = slice(done * SIDE, (done + 2) * SIDE)
            result[0, :, at] = jnp.where(lower, even, pltpu.roll(odd, SIDE, 1))
            result[1, :, at] = jnp.where(lower, pltpu.roll(even, SIDE, 1), odd)
            done += 2
            if done % part == 0:
                n = done // part - 1
                at = slice(n * part * SIDE, (n + 1) * part * SIDE)
                for tile in range(2):
                    copy = pltpu.make_async_copy(
                        result.at[tile, :, at], out.at[tile, :, at], sems.at[tile, n]
                    )
                    copy.start()
                    copies.append(copy)
    for copy in copies:
        copy.wait()


def convolutions(field, above, below, links, weight1, weight2, scale, bias, out_bias):
    channels = field.shape[0]
    stack = pltpu.VMEM((3 * channels, (SIDE + 2) * 128), BF)
    return pl.pallas_call(
        conv_kernel,
        out_shape=jax.ShapeDtypeStruct((2, channels, CELLS), F32),
        in_specs=[VMEM, VMEM, VMEM, SMEM] + [VMEM] * 5,
        out_specs=pl.BlockSpec(memory_space=pl.ANY),
        scratch_shapes=[
            stack,
            stack,
            pltpu.VMEM((3 * channels, 768), BF),
            pltpu.VMEM((2, channels, CELLS), F32),
            pltpu.SemaphoreType.DMA((2, 4)),
        ],
        compiler_params=params(44),
    )(field, above, below, links, weight1, weight2, scale, bias, out_bias)


def exchange(tops, bottoms):
    devices = lax.axis_size("dev")
    above = lax.ppermute(bottoms, "dev", [(i, i + 1) for i in range(devices - 1)])
    below = lax.ppermute(tops, "dev", [(i + 1, i) for i in range(devices - 1)])
    return above, below


def by_row_tap(weight):
    channels = weight.shape[0]
    return weight.reshape(channels, 3, 3 * channels).transpose(1, 0, 2).reshape(3 * channels, -1)


def per_device(
    context,
    depth_logits,
    send_point,
    recv_cell,
    neighbour,
    conv1_weight,
    layer_scale,
    layer_bias,
    conv2_weight,
    out_bias,
):
    lifted = lift(context, depth_logits, send_point[0])
    arrived = lax.all_to_all(lifted, "dev", split_axis=0, concat_axis=0, tiled=True)
    bev, tops, bottoms = splat(arrived, recv_cell[0])
    above, below = exchange(tops, bottoms)
    out = convolutions(
        bev,
        above,
        below,
        neighbour[0],
        by_row_tap(conv1_weight),
        by_row_tap(conv2_weight),
        layer_scale[:, None],
        layer_bias[:, None],
        out_bias[:, None],
    )
    return out[None]


def solution(mesh):
    in_specs = (
        P(None, "dev"),
        P(None, "dev"),
        P("dev", None, None),
        P("dev", None, None),
        P("dev", None, None),
        P(),
        P(),
        P(),
        P(),
        P(),
    )
    out_specs = P("dev", None, None, None)
    return jax.shard_map(
        per_device, mesh=mesh, in_specs=in_specs, out_specs=out_specs, check_vma=False
    )
```

```python
import functools

import jax
import jax.numpy as jnp
from jax import lax
from jax.experimental import pallas as pl
from jax.experimental.pallas import tpu as pltpu
from jax.sharding import PartitionSpec as P

SIDE = 64
CELLS = SIDE * SIDE
BF = jnp.bfloat16
F32 = jnp.float32
VMEM = pl.BlockSpec(memory_space=pltpu.VMEM)
SMEM = pl.BlockSpec(memory_space=pltpu.SMEM)


def params(megabytes):
    return pltpu.CompilerParams(vmem_limit_bytes=megabytes * 1024 * 1024)


def float_iota(shape, axis):
    return lax.broadcasted_iota(jnp.int32, shape, axis).astype(F32).astype(BF)


def split_high(value):
    high = value.astype(BF).astype(F32)
    return high, value - high


def lift_kernel(unroll, context_in, logits_in, send_in, out, lifted, context, logits, send, wide, table, sems):
    pairs = ((logits_in, logits), (context_in, context), (send_in, send))
    copies = [pltpu.make_async_copy(a, b, sems.at[n]) for n, (a, b) in enumerate(pairs)]
    for copy in copies:
        copy.start()
    channels, pixels = context.shape
    depths = logits.shape[0]
    slots = send.shape[1]
    bins = -(-depths // 8) * 8
    copies[0].wait()
    values = logits[...].astype(F32)
    largest = jnp.max(values, axis=0, keepdims=True)
    inverse = 1.0 / jnp.sum(jnp.exp(values - largest), axis=0, keepdims=True)
    wide[...] = jnp.zeros(wide.shape, F32)
    wide[0:depths, :] = values
    wide[bins : bins + 1, :] = largest
    for n in range(3):
        high, inverse = split_high(inverse)
        wide[bins + 1 + n : bins + 2 + n, :] = high
    copies[1].wait()
    copies[2].wait()
    table[0:channels, :] = context[...]
    table[channels:, :] = wide[...].astype(BF)
    pixel_iota = float_iota((pixels, slots), 0)
    bin_iota = lax.broadcasted_iota(jnp.int32, (8, slots), 0)
    one, zero = jnp.ones((), BF), jnp.zeros((), BF)

    def step(i, carry):
        points = [send[pl.ds(i * unroll + u, 1), :] for u in range(unroll)]
        picks = []
        for point in points:
            pixel = (point & (pixels - 1)).astype(F32).astype(BF)
            picks.append(jnp.where(pixel_iota == pixel, one, zero))
        for v in range(0, unroll, 2):
            found = jnp.dot(
                table[...], jnp.concatenate(picks[v : v + 2], axis=1), preferred_element_type=F32
            )
            for u in (v, v + 1):
                point = points[u]
                mine = found[:, (u - v) * slots : (u - v + 1) * slots]
                offset = (point >> 8) - bin_iota
                chosen = jnp.zeros((8, slots), F32)
                for r in range(0, bins, 8):
                    chosen = jnp.where(offset == r, mine[channels + r : channels + r + 8], chosen)
                logit = jnp.sum(chosen, axis=0, keepdims=True)
                tail = mine[channels + bins :]
                scale = tail[1:2] + tail[2:3] + tail[3:4]
                weight = jnp.exp(logit - tail[0:1]) * scale
                weight = jnp.where(point >= 0, weight, 0.0)
                lifted[i * unroll + u] = (mine[0:channels] * weight).astype(BF)
        leave(i).start()
        return carry

    def leave(i):
        at = pl.ds(i * unroll, unroll)
        return pltpu.make_async_copy(lifted.at[at], out.at[at], sems.at[3 + i])

    lax.fori_loop(0, send.shape[0] // unroll, step, 0)
    for i in range(send.shape[0] // unroll):
        leave(i).wait()


def lift(context, logits, send):
    channels, pixels = context.shape
    return pl.pallas_call(
        functools.partial(lift_kernel, 32),
        out_shape=jax.ShapeDtypeStruct((send.shape[0], channels, send.shape[1]), BF),
        in_specs=[pl.BlockSpec(memory_space=pl.ANY)] * 3,
        out_specs=pl.BlockSpec(memory_space=pl.ANY),
        scratch_shapes=[
            pltpu.VMEM((send.shape[0], channels, send.shape[1]), BF),
            pltpu.VMEM(context.shape, BF),
            pltpu.VMEM(logits.shape, BF),
            pltpu.VMEM(send.shape, jnp.int32),
            pltpu.VMEM((128, pixels), F32),
            pltpu.VMEM((channels + 128, pixels), BF),
            pltpu.SemaphoreType.DMA((3 + send.shape[0] // 32,)),
        ],
        compiler_params=params(60),
    )(context, logits, send)


def field_edges(field, tops, bottoms):
    tops[...] = field[:, 0:256]
    bottoms[...] = field[:, 2 * CELLS - 256 : 2 * CELLS]


def field_place(cell):
    row, x = (cell >> 6) & (SIDE - 1), cell & (SIDE - 1)
    return jnp.where(cell < 0, -1, row * 128 + (cell >> 12) * SIDE + x)


def list_starts(cells):
    half = (cells >> 11) & 1
    counts = jnp.stack([jnp.sum((cells >= 0) & (half == n), axis=1, dtype=jnp.int32) for n in range(2)])
    return jnp.pad(jnp.cumsum(counts, axis=1), ((0, 0), (1, 0)))


def start_of(starts, n, s):
    first, last = starts[n, s], starts[n, s + 1]
    return first >> 7, first & 127, (last >> 7) > (first >> 7)


def plan_kernel(unroll, cells, starts, index, places, ranks, current):
    sources, slots = cells.shape
    below = lax.broadcasted_iota(jnp.int32, (slots, slots), 0)
    after = lax.broadcasted_iota(jnp.int32, (slots, slots), 1)
    earlier = jnp.where(below < after, 1.0, 0.0).astype(BF)
    cell = cells[...]
    for n in range(2):
        member = jnp.where((cell >= 0) & (((cell >> 11) & 1) == n), 1.0, 0.0).astype(BF)
        found = jnp.dot(member, earlier, preferred_element_type=F32)
        ranks[n] = jnp.where(member.astype(F32) > 0.5, found, -1.0).astype(jnp.int32)
        places[n] = jnp.full(places.shape[1:], -1, jnp.int32)
    current[...] = jnp.full(current.shape, -1, jnp.int32)
    slot_iota = float_iota((slots, slots), 0)
    which = lax.broadcasted_iota(jnp.int32, (16, slots), 0)
    lane = lax.broadcasted_iota(jnp.int32, (1, slots), 1)
    one, zero = jnp.ones((), BF), jnp.zeros((), BF)

    def step(i, carry):
        for u in range(unroll):
            s = i * unroll + u
            place = field_place(cells[pl.ds(s, 1), :]) + 1
            rows = jnp.where(which == 0, lane, jnp.where(which == 1, place >> 6, place & 63))
            picks = []
            for n in range(2):
                rank = ranks[n, pl.ds(s, 1), :]
                _, offset, _ = start_of(starts, n, s)
                to = jnp.where(rank < 0, -1, (rank + offset) & 127).astype(F32).astype(BF)
                picks.append(jnp.where(slot_iota == to, one, zero))
            found = lax.dot_general(
                rows.astype(F32).astype(BF),
                jnp.concatenate(picks, axis=0),
                (((1,), (1,)), ((), ())),
                preferred_element_type=F32,
            ).astype(jnp.int32)
            for n in range(2):
                mine = found[:, n * slots : (n + 1) * slots]
                block, offset, full = start_of(starts, n, s)
                index[n, pl.ds(s, 1), :] = mine[0:1]
                place = mine[1:2] * 64 + mine[2:3] - 1
                stored = jnp.where(lane >= offset, place, current[n : n + 1, :])
                places[n, pl.ds(block, 1), :] = stored
                current[n : n + 1, :] = jnp.where(full, place, stored)
        return carry

    lax.fori_loop(0, sources // unroll, step, 0)
    for n in range(2):
        total = starts[n, sources]
        places[n, pl.ds(total >> 7, 1), :] = jnp.where(lane < (total & 127), current[n : n + 1, :], -1)


LIST_BLOCK = 22


def plan(cells, starts):
    sources, slots = cells.shape
    blocks = sources + 2 * LIST_BLOCK
    return pl.pallas_call(
        functools.partial(plan_kernel, 16),
        out_shape=(
            jax.ShapeDtypeStruct((2, sources, slots), jnp.int32),
            jax.ShapeDtypeStruct((2, blocks, slots), jnp.int32),
        ),
        in_specs=[VMEM, SMEM],
        out_specs=(VMEM, VMEM),
        scratch_shapes=[pltpu.VMEM((2, sources, slots), jnp.int32), pltpu.VMEM((8, slots), jnp.int32)],
        compiler_params=params(16),
        cost_estimate=pl.CostEstimate(flops=10**9, bytes_accessed=10**6, transcendentals=0),
    )(cells, starts)


def splat_kernel(
    groups, unroll, arrived, index, places, starts, out, tops, bottoms, lists, total, bev, sems
):
    sources, channels, slots = arrived.shape
    width = total.shape[2]
    shift = width.bit_length() - 1
    lane = lax.broadcasted_iota(jnp.int32, (channels, slots), 1)
    nothing = jnp.zeros((channels, slots), F32)

    def put(n, block, value):
        lists[n, :, pl.ds(pl.multiple_of(block * slots, slots), slots)] = value.astype(BF)

    def gather(i, carry):
        carry = list(carry)
        for u in range(unroll):
            s = i * unroll + u
            values = arrived[s].astype(F32)
            for n in range(2):
                block, offset, full = start_of(starts, n, s)
                source = jnp.broadcast_to(index[n, pl.ds(s, 1), :], values.shape)
                moved = jnp.take_along_axis(values, source, axis=1, mode="promise_in_bounds")
                stored = jnp.where(lane >= offset, moved, carry[n])
                put(n, block, stored)
                carry[n] = jnp.where(full, moved, stored)
        return tuple(carry)

    rest = lax.fori_loop(0, sources // unroll, gather, (nothing, nothing))
    for n in range(2):
        end = starts[n, sources] >> 7
        put(n, end, rest[n])
        for b in range(1, LIST_BLOCK + 1):
            put(n, end + b, nothing)
    total[...] = jnp.zeros(total.shape, F32)
    span = slots * LIST_BLOCK
    block = 256
    cell_iota = float_iota((block, span), 0)
    one, zero = jnp.ones((), BF), jnp.zeros((), BF)
    copies = []
    for n in range(2):

        def step(i, carry):
            values = lists[n, :, pl.ds(pl.multiple_of(i * span, span), span)]
            rows = [places[n, pl.ds(i * LIST_BLOCK + u, 1), :] for u in range(LIST_BLOCK)]
            target = jnp.concatenate(rows, axis=1)
            target = jnp.where(target < 0, -1, target - n * CELLS)
            group = target >> shift
            place = target & (width - 1)
            masked = [values * jnp.where(group == g, 1.0, 0.0).astype(BF) for g in range(groups)]
            grouped = jnp.concatenate(masked, axis=0)
            for j in range(width // block):
                spot = (place - j * block).astype(F32).astype(BF)
                pick = jnp.where(cell_iota == spot, one, zero)
                total[n, :, j * block : (j + 1) * block] += lax.dot_general(
                    grouped, pick, (((1,), (1,)), ((), ())), preferred_element_type=F32
                )
            return carry

        lax.fori_loop(0, (starts[n, sources] + span - 1) // span, step, 0)
        for g in range(groups):
            at = slice(n * CELLS + g * width, n * CELLS + (g + 1) * width)
            bev[:, at] = total[n, g * channels : (g + 1) * channels, :].astype(BF)
        at = slice(n * CELLS, (n + 1) * CELLS)
        copies.append(pltpu.make_async_copy(bev.at[:, at], out.at[:, at], sems.at[n]))
        copies[n].start()
    field_edges(bev, tops, bottoms)
    for copy in copies:
        copy.wait()


def splat(arrived, index, places, starts):
    sources, channels, slots = arrived.shape
    groups = 4
    edge = jax.ShapeDtypeStruct((channels, 256), BF)
    return pl.pallas_call(
        functools.partial(splat_kernel, groups, 16),
        out_shape=(jax.ShapeDtypeStruct((channels, 2 * CELLS), BF), edge, edge),
        in_specs=[VMEM, VMEM, VMEM, SMEM],
        out_specs=(pl.BlockSpec(memory_space=pl.ANY), VMEM, VMEM),
        scratch_shapes=[
            pltpu.VMEM((2, channels, (sources + 2 * LIST_BLOCK) * slots), BF),
            pltpu.VMEM((2, groups * channels, CELLS // groups), F32),
            pltpu.VMEM((channels, 2 * CELLS), BF),
            pltpu.SemaphoreType.DMA((2,)),
        ],
        compiler_params=params(32),
    )(arrived, index, places, starts)


def conv_kernel(
    field,
    above,
    below,
    links,
    weight1,
    weight2,
    scale,
    bias,
    out_bias,
    out,
    stack1,
    stack2,
    side_stack,
    result,
    sems,
):
    channels = field.shape[0]
    shape = (channels, 128)
    lane = lax.broadcasted_iota(jnp.int32, shape, 1)
    lower = lane < SIDE
    column = lane & (SIDE - 1)

    def gate(tile, n, want):
        return jnp.where(links[tile, n] == want, 1.0, 0.0)

    def block(ref, y):
        return ref[:, y * 128 : (y + 1) * 128]

    def put(stack, slot, left, center, right):
        for b, image in enumerate((left, center, right)):
            stack[b * channels : (b + 1) * channels, slot * 128 : (slot + 1) * 128] = image.astype(BF)

    def keeps(joined):
        left = jnp.where(lane == 0, 0.0, jnp.where(lane == SIDE, joined, 1.0))
        right = jnp.where(lane == 127, 0.0, jnp.where(lane == SIDE - 1, joined, 1.0))
        return left, right

    def put_row(stack, slot, row, keep):
        wide = row.astype(F32)
        put(stack, slot, pltpu.roll(wide, 1, 1) * keep[0], row, pltpu.roll(wide, 127, 1) * keep[1])

    def put_mapped(stack, slot, source, west, center, east, inverse=False):
        swapped = pltpu.roll(source, SIDE, 1)

        def mapped(n):
            cross = [gate(0, n, 1), gate(1, n, 0)]
            if inverse:
                cross.reverse()
            same = jnp.where(lower, gate(0, n, 0), gate(1, n, 1))
            return source * same + swapped * jnp.where(lower, cross[0], cross[1])

        middle = mapped(center)
        left = jnp.where(column == 0, pltpu.roll(mapped(west), SIDE + 1, 1), pltpu.roll(middle, 1, 1))
        right = jnp.where(
            column == SIDE - 1, pltpu.roll(mapped(east), SIDE - 1, 1), pltpu.roll(middle, 127, 1)
        )
        put(stack, slot, left, middle, right)

    def multiply(weight, stack, product, start, stop):
        found = jnp.dot(
            weight[...], stack[:, start * 128 : stop * 128], preferred_element_type=F32
        )
        for slot in range(start, stop):
            lanes = slice((slot - start) * 128, (slot - start + 1) * 128)
            for a in range(3):
                product[a, slot] = found[a * channels : (a + 1) * channels, lanes]

    def summed(product, slots):
        first, second, third = (product.pop((a, slot)) for a, slot in enumerate(slots))
        return first + second + third

    def joined(west, center, east):
        found = 0.0
        for j in range(2):
            for a, b in ((west, center), (center, east)):
                found = jnp.maximum(found, gate(j, a, 0) * gate(j, b, 1))
        return found

    gain = jnp.broadcast_to(scale[...], shape)
    shift = jnp.broadcast_to(bias[...], shape)
    last_shift = jnp.broadcast_to(out_bias[...], shape)
    keep = keeps(gate(1, 3, 0))
    keep_up, keep_down = keeps(joined(0, 1, 2)), keeps(joined(5, 6, 7))
    end = SIDE + 1
    product1, product2, side_product = {}, {}, {}

    def activate(value):
        return jnp.maximum(gain * value + shift, 0.0).astype(BF)

    put_row(side_stack, 0, block(above, 0), keep_up)
    put_row(side_stack, 1, block(above, 1), keep_up)
    put_mapped(side_stack, 2, block(field, 0).astype(F32), 2, 1, 0, True)
    put_mapped(side_stack, 3, block(field, SIDE - 1).astype(F32), 7, 6, 5, True)
    put_row(side_stack, 4, block(below, 0), keep_down)
    put_row(side_stack, 5, block(below, 1), keep_down)
    multiply(weight1, side_stack, side_product, 0, 6)
    up_row = activate(summed(side_product, (0, 1, 2))).astype(F32)
    down_row = activate(summed(side_product, (3, 4, 5))).astype(F32)
    put_mapped(stack2, 0, up_row, 0, 1, 2)
    put_mapped(stack2, end, down_row, 5, 6, 7)
    put_mapped(stack1, 0, block(above, 1).astype(F32), 0, 1, 2)
    put_mapped(stack1, end, block(below, 0).astype(F32), 5, 6, 7)

    step = 16
    done = 0
    for start in range(0, SIDE + 2, step):
        stop = min(start + step, SIDE + 2)
        for slot in range(max(start, 1), min(stop, end)):
            put_row(stack1, slot, block(field, slot - 1), keep)
        multiply(weight1, stack1, product1, start, stop)
        while done < stop - 2:
            put_row(stack2, done + 1, activate(summed(product1, (done, done + 1, done + 2))), keep)
            done += 1

    copies = []
    done = 0
    part = 16
    for start in range(0, SIDE + 2, step):
        stop = min(start + step, SIDE + 2)
        multiply(weight2, stack2, product2, start, stop)
        while done + 1 < stop - 2:
            even = summed(product2, (done, done + 1, done + 2)) + last_shift
            odd = summed(product2, (done + 1, done + 2, done + 3)) + last_shift
            at = slice(done * SIDE, (done + 2) * SIDE)
            result[0, :, at] = jnp.where(lower, even, pltpu.roll(odd, SIDE, 1))
            result[1, :, at] = jnp.where(lower, pltpu.roll(even, SIDE, 1), odd)
            done += 2
            if done % part == 0:
                n = done // part - 1
                at = slice(n * part * SIDE, (n + 1) * part * SIDE)
                for tile in range(2):
                    copy = pltpu.make_async_copy(
                        result.at[tile, :, at], out.at[tile, :, at], sems.at[tile, n]
                    )
                    copy.start()
                    copies.append(copy)
    for copy in copies:
        copy.wait()


def convolutions(field, above, below, links, weight1, weight2, scale, bias, out_bias):
    channels = field.shape[0]
    stack = pltpu.VMEM((3 * channels, (SIDE + 2) * 128), BF)
    return pl.pallas_call(
        conv_kernel,
        out_shape=jax.ShapeDtypeStruct((2, channels, CELLS), F32),
        in_specs=[VMEM, VMEM, VMEM, SMEM] + [VMEM] * 5,
        out_specs=pl.BlockSpec(memory_space=pl.ANY),
        scratch_shapes=[
            stack,
            stack,
            pltpu.VMEM((3 * channels, 768), BF),
            pltpu.VMEM((2, channels, CELLS), F32),
            pltpu.SemaphoreType.DMA((2, 4)),
        ],
        compiler_params=params(44),
    )(field, above, below, links, weight1, weight2, scale, bias, out_bias)


def exchange(tops, bottoms):
    devices = lax.axis_size("dev")
    above = lax.ppermute(bottoms, "dev", [(i, i + 1) for i in range(devices - 1)])
    below = lax.ppermute(tops, "dev", [(i + 1, i) for i in range(devices - 1)])
    return above, below


def by_row_tap(weight):
    channels = weight.shape[0]
    return weight.reshape(channels, 3, 3 * channels).transpose(1, 0, 2).reshape(3 * channels, -1)


def per_device(
    context,
    depth_logits,
    send_point,
    recv_cell,
    neighbour,
    conv1_weight,
    layer_scale,
    layer_bias,
    conv2_weight,
    out_bias,
):
    lifted = lift(context, depth_logits, send_point[0])
    arrived = lax.all_to_all(lifted, "dev", split_axis=0, concat_axis=0, tiled=True)
    starts = list_starts(recv_cell[0])
    index, places = plan(recv_cell[0], starts)
    bev, tops, bottoms = splat(arrived, index, places, starts)
    above, below = exchange(tops, bottoms)
    out = convolutions(
        bev,
        above,
        below,
        neighbour[0],
        by_row_tap(conv1_weight),
        by_row_tap(conv2_weight),
        layer_scale[:, None],
        layer_bias[:, None],
        out_bias[:, None],
    )
    return out[None]


def solution(mesh):
    in_specs = (
        P(None, "dev"),
        P(None, "dev"),
        P("dev", None, None),
        P("dev", None, None),
        P("dev", None, None),
        P(),
        P(),
        P(),
        P(),
        P(),
    )
    out_specs = P("dev", None, None, None)
    return jax.shard_map(
        per_device, mesh=mesh, in_specs=in_specs, out_specs=out_specs, check_vma=False
    )
```

```python
import functools

import jax
import jax.numpy as jnp
from jax import lax
from jax.experimental import pallas as pl
from jax.experimental.pallas import tpu as pltpu
from jax.sharding import PartitionSpec as P

SIDE = 64
CELLS = SIDE * SIDE
BF = jnp.bfloat16
F32 = jnp.float32
VMEM = pl.BlockSpec(memory_space=pltpu.VMEM)
SMEM = pl.BlockSpec(memory_space=pltpu.SMEM)


def params(megabytes):
    return pltpu.CompilerParams(vmem_limit_bytes=megabytes * 1024 * 1024)


def float_iota(shape, axis):
    return lax.broadcasted_iota(jnp.int32, shape, axis).astype(F32).astype(BF)


def split_high(value):
    high = value.astype(BF).astype(F32)
    return high, value - high


def lift_kernel(unroll, context_in, logits_in, send_in, out, lifted, context, logits, send, wide, table, sems):
    pairs = ((logits_in, logits), (context_in, context), (send_in, send))
    copies = [pltpu.make_async_copy(a, b, sems.at[n]) for n, (a, b) in enumerate(pairs)]
    for copy in copies:
        copy.start()
    channels, pixels = context.shape
    depths = logits.shape[0]
    slots = send.shape[1]
    bins = -(-depths // 8) * 8
    copies[0].wait()
    values = logits[...].astype(F32)
    largest = jnp.max(values, axis=0, keepdims=True)
    inverse = 1.0 / jnp.sum(jnp.exp(values - largest), axis=0, keepdims=True)
    wide[...] = jnp.zeros(wide.shape, F32)
    wide[0:depths, :] = values
    wide[bins : bins + 1, :] = largest
    for n in range(3):
        high, inverse = split_high(inverse)
        wide[bins + 1 + n : bins + 2 + n, :] = high
    copies[1].wait()
    copies[2].wait()
    table[0:channels, :] = context[...]
    table[channels:, :] = wide[...].astype(BF)
    pixel_iota = float_iota((pixels, slots), 0)
    bin_iota = lax.broadcasted_iota(jnp.int32, (8, slots), 0)
    one, zero = jnp.ones((), BF), jnp.zeros((), BF)

    def step(i, carry):
        points = [send[pl.ds(i * unroll + u, 1), :] for u in range(unroll)]
        picks = []
        for point in points:
            pixel = (point & (pixels - 1)).astype(F32).astype(BF)
            picks.append(jnp.where(pixel_iota == pixel, one, zero))
        for v in range(0, unroll, 2):
            found = jnp.dot(
                table[...], jnp.concatenate(picks[v : v + 2], axis=1), preferred_element_type=F32
            )
            for u in (v, v + 1):
                point = points[u]
                mine = found[:, (u - v) * slots : (u - v + 1) * slots]
                offset = (point >> 8) - bin_iota
                chosen = jnp.zeros((8, slots), F32)
                for r in range(0, bins, 8):
                    chosen = jnp.where(offset == r, mine[channels + r : channels + r + 8], chosen)
                logit = jnp.sum(chosen, axis=0, keepdims=True)
                tail = mine[channels + bins :]
                scale = tail[1:2] + tail[2:3] + tail[3:4]
                weight = jnp.exp(logit - tail[0:1]) * scale
                weight = jnp.where(point >= 0, weight, 0.0)
                lifted[i * unroll + u] = (mine[0:channels] * weight).astype(BF)
        leave(i).start()
        return carry

    def leave(i):
        at = pl.ds(i * unroll, unroll)
        return pltpu.make_async_copy(lifted.at[at], out.at[at], sems.at[3 + i])

    lax.fori_loop(0, send.shape[0] // unroll, step, 0)
    for i in range(send.shape[0] // unroll):
        leave(i).wait()


def lift(context, logits, send):
    channels, pixels = context.shape
    return pl.pallas_call(
        functools.partial(lift_kernel, 32),
        out_shape=jax.ShapeDtypeStruct((send.shape[0], channels, send.shape[1]), BF),
        in_specs=[pl.BlockSpec(memory_space=pl.ANY)] * 3,
        out_specs=pl.BlockSpec(memory_space=pl.ANY),
        scratch_shapes=[
            pltpu.VMEM((send.shape[0], channels, send.shape[1]), BF),
            pltpu.VMEM(context.shape, BF),
            pltpu.VMEM(logits.shape, BF),
            pltpu.VMEM(send.shape, jnp.int32),
            pltpu.VMEM((128, pixels), F32),
            pltpu.VMEM((channels + 128, pixels), BF),
            pltpu.SemaphoreType.DMA((3 + send.shape[0] // 32,)),
        ],
        compiler_params=params(60),
    )(context, logits, send)


def field_edges(field, tops, bottoms):
    tops[...] = field[:, 0:256]
    bottoms[...] = field[:, 2 * CELLS - 256 : 2 * CELLS]


def field_place(cell):
    row, x = (cell >> 6) & (SIDE - 1), cell & (SIDE - 1)
    return jnp.where(cell < 0, -1, row * 128 + (cell >> 12) * SIDE + x)


def list_starts(cells):
    half = (cells >> 11) & 1
    counts = jnp.stack([jnp.sum((cells >= 0) & (half == n), axis=1, dtype=jnp.int32) for n in range(2)])
    return jnp.pad(jnp.cumsum(counts, axis=1), ((0, 0), (1, 0)))


def start_of(starts, n, s):
    first, last = starts[n, s], starts[n, s + 1]
    return first >> 7, first & 127, (last >> 7) > (first >> 7)


def plan_kernel(unroll, cells, starts, index, places, ranks, current):
    sources, slots = cells.shape
    below = lax.broadcasted_iota(jnp.int32, (slots, slots), 0)
    after = lax.broadcasted_iota(jnp.int32, (slots, slots), 1)
    earlier = jnp.where(below < after, 1.0, 0.0).astype(BF)
    cell = cells[...]
    for n in range(2):
        member = jnp.where((cell >= 0) & (((cell >> 11) & 1) == n), 1.0, 0.0).astype(BF)
        found = jnp.dot(member, earlier, preferred_element_type=F32)
        ranks[n] = jnp.where(member.astype(F32) > 0.5, found, -1.0).astype(jnp.int32)
        places[n] = jnp.full(places.shape[1:], -1, jnp.int32)
    current[...] = jnp.full(current.shape, -1, jnp.int32)
    slot_iota = float_iota((slots, slots), 0)
    which = lax.broadcasted_iota(jnp.int32, (16, slots), 0)
    lane = lax.broadcasted_iota(jnp.int32, (1, slots), 1)
    one, zero = jnp.ones((), BF), jnp.zeros((), BF)

    def step(i, carry):
        for u in range(unroll):
            s = i * unroll + u
            place = field_place(cells[pl.ds(s, 1), :]) + 1
            rows = jnp.where(which == 0, lane, jnp.where(which == 1, place >> 6, place & 63))
            picks = []
            for n in range(2):
                rank = ranks[n, pl.ds(s, 1), :]
                _, offset, _ = start_of(starts, n, s)
                to = jnp.where(rank < 0, -1, (rank + offset) & 127).astype(F32).astype(BF)
                picks.append(jnp.where(slot_iota == to, one, zero))
            found = lax.dot_general(
                rows.astype(F32).astype(BF),
                jnp.concatenate(picks, axis=0),
                (((1,), (1,)), ((), ())),
                preferred_element_type=F32,
            ).astype(jnp.int32)
            for n in range(2):
                mine = found[:, n * slots : (n + 1) * slots]
                block, offset, full = start_of(starts, n, s)
                index[n, pl.ds(s, 1), :] = mine[0:1]
                place = mine[1:2] * 64 + mine[2:3] - 1
                stored = jnp.where(lane >= offset, place, current[n : n + 1, :])
                places[n, pl.ds(block, 1), :] = stored
                current[n : n + 1, :] = jnp.where(full, place, stored)
        return carry

    lax.fori_loop(0, sources // unroll, step, 0)
    for n in range(2):
        total = starts[n, sources]
        places[n, pl.ds(total >> 7, 1), :] = jnp.where(lane < (total & 127), current[n : n + 1, :], -1)


LIST_BLOCK = 22


def plan(cells, starts):
    sources, slots = cells.shape
    blocks = sources + 2 * LIST_BLOCK
    return pl.pallas_call(
        functools.partial(plan_kernel, 16),
        out_shape=(
            jax.ShapeDtypeStruct((2, sources, slots), jnp.int32),
            jax.ShapeDtypeStruct((2, blocks, slots), jnp.int32),
        ),
        in_specs=[VMEM, SMEM],
        out_specs=(VMEM, VMEM),
        scratch_shapes=[pltpu.VMEM((2, sources, slots), jnp.int32), pltpu.VMEM((8, slots), jnp.int32)],
        compiler_params=params(16),
        cost_estimate=pl.CostEstimate(flops=10**9, bytes_accessed=10**6, transcendentals=0),
    )(cells, starts)


def splat_kernel(
    groups, unroll, arrived, index, places, starts, bev, tops, bottoms, lists, total
):
    sources, channels, slots = arrived.shape
    width = total.shape[2]
    shift = width.bit_length() - 1
    lane = lax.broadcasted_iota(jnp.int32, (channels, slots), 1)
    nothing = jnp.zeros((channels, slots), F32)

    def put(n, block, value):
        lists[n, :, pl.ds(pl.multiple_of(block * slots, slots), slots)] = value.astype(BF)

    def gather(i, carry):
        carry = list(carry)
        for u in range(unroll):
            s = i * unroll + u
            values = arrived[s].astype(F32)
            for n in range(2):
                block, offset, full = start_of(starts, n, s)
                source = jnp.broadcast_to(index[n, pl.ds(s, 1), :], values.shape)
                moved = jnp.take_along_axis(values, source, axis=1, mode="promise_in_bounds")
                stored = jnp.where(lane >= offset, moved, carry[n])
                put(n, block, stored)
                carry[n] = jnp.where(full, moved, stored)
        return tuple(carry)

    rest = lax.fori_loop(0, sources // unroll, gather, (nothing, nothing))
    for n in range(2):
        end = starts[n, sources] >> 7
        put(n, end, rest[n])
        for b in range(1, LIST_BLOCK + 1):
            put(n, end + b, nothing)
    total[...] = jnp.zeros(total.shape, F32)
    span = slots * LIST_BLOCK
    block = 256
    cell_iota = float_iota((block, span), 0)
    one, zero = jnp.ones((), BF), jnp.zeros((), BF)
    for n in range(2):

        def step(i, carry):
            values = lists[n, :, pl.ds(pl.multiple_of(i * span, span), span)]
            rows = [places[n, pl.ds(i * LIST_BLOCK + u, 1), :] for u in range(LIST_BLOCK)]
            target = jnp.concatenate(rows, axis=1)
            target = jnp.where(target < 0, -1, target - n * CELLS)
            group = target >> shift
            place = target & (width - 1)
            masked = [values * jnp.where(group == g, 1.0, 0.0).astype(BF) for g in range(groups)]
            grouped = jnp.concatenate(masked, axis=0)
            for j in range(width // block):
                spot = (place - j * block).astype(F32).astype(BF)
                pick = jnp.where(cell_iota == spot, one, zero)
                total[n, :, j * block : (j + 1) * block] += lax.dot_general(
                    grouped, pick, (((1,), (1,)), ((), ())), preferred_element_type=F32
                )
            return carry

        lax.fori_loop(0, (starts[n, sources] + span - 1) // span, step, 0)
        for g in range(groups):
            at = slice(n * CELLS + g * width, n * CELLS + (g + 1) * width)
            bev[:, at] = total[n, g * channels : (g + 1) * channels, :].astype(BF)
    field_edges(bev, tops, bottoms)


def splat(arrived, index, places, starts):
    sources, channels, slots = arrived.shape
    groups = 4
    edge = jax.ShapeDtypeStruct((channels, 256), BF)
    return pl.pallas_call(
        functools.partial(splat_kernel, groups, 16),
        out_shape=(jax.ShapeDtypeStruct((channels, 2 * CELLS), BF), edge, edge),
        in_specs=[VMEM, VMEM, VMEM, SMEM],
        out_specs=(VMEM,) * 3,
        scratch_shapes=[
            pltpu.VMEM((2, channels, (sources + 2 * LIST_BLOCK) * slots), BF),
            pltpu.VMEM((2, groups * channels, CELLS // groups), F32),
        ],
        compiler_params=params(32),
    )(arrived, index, places, starts)


def prepare_kernel(conv1, conv2, scale, bias, out_bias, weight1, weight2, vectors, square):
    channels, taps = scale.shape[1], weight1.shape[0]
    for source, target in ((conv1, weight1), (conv2, weight2)):
        for a in range(3):
            rows = source[:, a * taps : (a + 1) * taps]
            target[a * channels : (a + 1) * channels, :] = rows
    square[...] = jnp.zeros(square.shape, F32)
    for n, vector in enumerate((scale, bias, out_bias)):
        square[:, 0:channels] = jnp.broadcast_to(vector[...], (square.shape[0], channels))
        vectors[n] = jnp.transpose(square[...])[0:channels, :]


def prepare(conv1, conv2, scale, bias, out_bias):
    channels = conv1.shape[0]
    weight = jax.ShapeDtypeStruct((3 * channels, 3 * channels), BF)
    return pl.pallas_call(
        prepare_kernel,
        out_shape=(weight, weight, jax.ShapeDtypeStruct((3, channels, 128), F32)),
        in_specs=[VMEM] * 5,
        out_specs=(VMEM,) * 3,
        scratch_shapes=[pltpu.VMEM((128, 128), F32)],
        compiler_params=params(16),
        cost_estimate=pl.CostEstimate(flops=10**8, bytes_accessed=10**6, transcendentals=0),
    )(conv1, conv2, scale[None], bias[None], out_bias[None])


def conv_kernel(
    field,
    above,
    below,
    links,
    weight1,
    weight2,
    vectors,
    out,
    stack1,
    stack2,
    side_stack,
    result,
    sems,
):
    channels = field.shape[0]
    shape = (channels, 128)
    lane = lax.broadcasted_iota(jnp.int32, shape, 1)
    lower = lane < SIDE
    column = lane & (SIDE - 1)

    def gate(tile, n, want):
        return jnp.where(links[tile, n] == want, 1.0, 0.0)

    def block(ref, y):
        return ref[:, y * 128 : (y + 1) * 128]

    def put(stack, slot, left, center, right):
        for b, image in enumerate((left, center, right)):
            stack[b * channels : (b + 1) * channels, slot * 128 : (slot + 1) * 128] = image.astype(BF)

    def keeps(joined):
        left = jnp.where(lane == 0, 0.0, jnp.where(lane == SIDE, joined, 1.0))
        right = jnp.where(lane == 127, 0.0, jnp.where(lane == SIDE - 1, joined, 1.0))
        return left, right

    def put_row(stack, slot, row, keep):
        wide = row.astype(F32)
        put(stack, slot, pltpu.roll(wide, 1, 1) * keep[0], row, pltpu.roll(wide, 127, 1) * keep[1])

    def put_mapped(stack, slot, source, west, center, east, inverse=False):
        swapped = pltpu.roll(source, SIDE, 1)

        def mapped(n):
            cross = [gate(0, n, 1), gate(1, n, 0)]
            if inverse:
                cross.reverse()
            same = jnp.where(lower, gate(0, n, 0), gate(1, n, 1))
            return source * same + swapped * jnp.where(lower, cross[0], cross[1])

        middle = mapped(center)
        left = jnp.where(column == 0, pltpu.roll(mapped(west), SIDE + 1, 1), pltpu.roll(middle, 1, 1))
        right = jnp.where(
            column == SIDE - 1, pltpu.roll(mapped(east), SIDE - 1, 1), pltpu.roll(middle, 127, 1)
        )
        put(stack, slot, left, middle, right)

    def multiply(weight, stack, product, start, stop):
        found = jnp.dot(
            weight[...], stack[:, start * 128 : stop * 128], preferred_element_type=F32
        )
        for slot in range(start, stop):
            lanes = slice((slot - start) * 128, (slot - start + 1) * 128)
            for a in range(3):
                product[a, slot] = found[a * channels : (a + 1) * channels, lanes]

    def summed(product, slots):
        first, second, third = (product.pop((a, slot)) for a, slot in enumerate(slots))
        return first + second + third

    def joined(west, center, east):
        found = 0.0
        for j in range(2):
            for a, b in ((west, center), (center, east)):
                found = jnp.maximum(found, gate(j, a, 0) * gate(j, b, 1))
        return found

    gain, shift, last_shift = (vectors[n] for n in range(3))
    keep = keeps(gate(1, 3, 0))
    keep_up, keep_down = keeps(joined(0, 1, 2)), keeps(joined(5, 6, 7))
    end = SIDE + 1
    product1, product2, side_product = {}, {}, {}

    def activate(value):
        return jnp.maximum(gain * value + shift, 0.0).astype(BF)

    put_row(side_stack, 0, block(above, 0), keep_up)
    put_row(side_stack, 1, block(above, 1), keep_up)
    put_mapped(side_stack, 2, block(field, 0).astype(F32), 2, 1, 0, True)
    put_mapped(side_stack, 3, block(field, SIDE - 1).astype(F32), 7, 6, 5, True)
    put_row(side_stack, 4, block(below, 0), keep_down)
    put_row(side_stack, 5, block(below, 1), keep_down)
    multiply(weight1, side_stack, side_product, 0, 6)
    up_row = activate(summed(side_product, (0, 1, 2))).astype(F32)
    down_row = activate(summed(side_product, (3, 4, 5))).astype(F32)
    put_mapped(stack2, 0, up_row, 0, 1, 2)
    put_mapped(stack2, end, down_row, 5, 6, 7)
    put_mapped(stack1, 0, block(above, 1).astype(F32), 0, 1, 2)
    put_mapped(stack1, end, block(below, 0).astype(F32), 5, 6, 7)

    step = 16
    done = 0
    for start in range(0, SIDE + 2, step):
        stop = min(start + step, SIDE + 2)
        for slot in range(max(start, 1), min(stop, end)):
            put_row(stack1, slot, block(field, slot - 1), keep)
        multiply(weight1, stack1, product1, start, stop)
        while done < stop - 2:
            put_row(stack2, done + 1, activate(summed(product1, (done, done + 1, done + 2))), keep)
            done += 1

    copies = []
    done = 0
    part = 16
    for start in range(0, SIDE + 2, step):
        stop = min(start + step, SIDE + 2)
        multiply(weight2, stack2, product2, start, stop)
        while done + 1 < stop - 2:
            even = summed(product2, (done, done + 1, done + 2)) + last_shift
            odd = summed(product2, (done + 1, done + 2, done + 3)) + last_shift
            at = slice(done * SIDE, (done + 2) * SIDE)
            result[0, :, at] = jnp.where(lower, even, pltpu.roll(odd, SIDE, 1))
            result[1, :, at] = jnp.where(lower, pltpu.roll(even, SIDE, 1), odd)
            done += 2
            if done % part == 0:
                n = done // part - 1
                at = slice(n * part * SIDE, (n + 1) * part * SIDE)
                for tile in range(2):
                    copy = pltpu.make_async_copy(
                        result.at[tile, :, at], out.at[tile, :, at], sems.at[tile, n]
                    )
                    copy.start()
                    copies.append(copy)
    for copy in copies:
        copy.wait()


def convolutions(field, above, below, links, weight1, weight2, vectors):
    channels = field.shape[0]
    stack = pltpu.VMEM((3 * channels, (SIDE + 2) * 128), BF)
    return pl.pallas_call(
        conv_kernel,
        out_shape=jax.ShapeDtypeStruct((2, channels, CELLS), F32),
        in_specs=[VMEM, VMEM, VMEM, SMEM] + [VMEM] * 3,
        out_specs=pl.BlockSpec(memory_space=pl.ANY),
        scratch_shapes=[
            stack,
            stack,
            pltpu.VMEM((3 * channels, 768), BF),
            pltpu.VMEM((2, channels, CELLS), F32),
            pltpu.SemaphoreType.DMA((2, 4)),
        ],
        compiler_params=params(44),
    )(field, above, below, links, weight1, weight2, vectors)


def exchange(tops, bottoms):
    devices = lax.axis_size("dev")
    above = lax.ppermute(bottoms, "dev", [(i, i + 1) for i in range(devices - 1)])
    below = lax.ppermute(tops, "dev", [(i + 1, i) for i in range(devices - 1)])
    return above, below


def per_device(
    context,
    depth_logits,
    send_point,
    recv_cell,
    neighbour,
    conv1_weight,
    layer_scale,
    layer_bias,
    conv2_weight,
    out_bias,
):
    lifted = lift(context, depth_logits, send_point[0])
    arrived = lax.all_to_all(lifted, "dev", split_axis=0, concat_axis=0, tiled=True)
    starts = list_starts(recv_cell[0])
    index, places = plan(recv_cell[0], starts)
    prepared = prepare(conv1_weight, conv2_weight, layer_scale, layer_bias, out_bias)
    places, prepared = lax.optimization_barrier((places, prepared))
    bev, tops, bottoms = splat(arrived, index, places, starts)
    above, below = exchange(tops, bottoms)
    out = convolutions(bev, above, below, neighbour[0], *prepared)
    return out[None]


def solution(mesh):
    in_specs = (
        P(None, "dev"),
        P(None, "dev"),
        P("dev", None, None),
        P("dev", None, None),
        P("dev", None, None),
        P(),
        P(),
        P(),
        P(),
        P(),
    )
    out_specs = P("dev", None, None, None)
    return jax.shard_map(
        per_device, mesh=mesh, in_specs=in_specs, out_specs=out_specs, check_vma=False
    )
```

```python
import functools

import jax
import jax.numpy as jnp
from jax import lax
from jax.experimental import pallas as pl
from jax.experimental.pallas import tpu as pltpu
from jax.sharding import PartitionSpec as P

SIDE = 64
CELLS = SIDE * SIDE
LISTS = 4
BF = jnp.bfloat16
F32 = jnp.float32
VMEM = pl.BlockSpec(memory_space=pltpu.VMEM)
SMEM = pl.BlockSpec(memory_space=pltpu.SMEM)


def params(megabytes):
    return pltpu.CompilerParams(vmem_limit_bytes=megabytes * 1024 * 1024)


def float_iota(shape, axis):
    return lax.broadcasted_iota(jnp.int32, shape, axis).astype(F32).astype(BF)


def split_high(value):
    high = value.astype(BF).astype(F32)
    return high, value - high


def lift_kernel(unroll, context_in, logits_in, send_in, out, lifted, context, logits, send, wide, table, sems):
    pairs = ((logits_in, logits), (context_in, context), (send_in, send))
    copies = [pltpu.make_async_copy(a, b, sems.at[n]) for n, (a, b) in enumerate(pairs)]
    for copy in copies:
        copy.start()
    channels, pixels = context.shape
    depths = logits.shape[0]
    slots = send.shape[1]
    bins = -(-depths // 8) * 8
    copies[0].wait()
    values = logits[...].astype(F32)
    largest = jnp.max(values, axis=0, keepdims=True)
    inverse = 1.0 / jnp.sum(jnp.exp(values - largest), axis=0, keepdims=True)
    wide[...] = jnp.zeros(wide.shape, F32)
    wide[0:depths, :] = values
    wide[bins : bins + 1, :] = largest
    for n in range(3):
        high, inverse = split_high(inverse)
        wide[bins + 1 + n : bins + 2 + n, :] = high
    copies[1].wait()
    copies[2].wait()
    table[0:channels, :] = context[...]
    table[channels:, :] = wide[...].astype(BF)
    pixel_iota = float_iota((pixels, slots), 0)
    bin_iota = lax.broadcasted_iota(jnp.int32, (8, slots), 0)
    one, zero = jnp.ones((), BF), jnp.zeros((), BF)

    def step(i, carry):
        points = [send[pl.ds(i * unroll + u, 1), :] for u in range(unroll)]
        picks = []
        for point in points:
            pixel = (point & (pixels - 1)).astype(F32).astype(BF)
            picks.append(jnp.where(pixel_iota == pixel, one, zero))
        for v in range(0, unroll, 2):
            found = jnp.dot(
                table[...], jnp.concatenate(picks[v : v + 2], axis=1), preferred_element_type=F32
            )
            for u in (v, v + 1):
                point = points[u]
                mine = found[:, (u - v) * slots : (u - v + 1) * slots]
                offset = (point >> 8) - bin_iota
                chosen = jnp.zeros((8, slots), F32)
                for r in range(0, bins, 8):
                    chosen = jnp.where(offset == r, mine[channels + r : channels + r + 8], chosen)
                logit = jnp.sum(chosen, axis=0, keepdims=True)
                tail = mine[channels + bins :]
                scale = tail[1:2] + tail[2:3] + tail[3:4]
                weight = jnp.exp(logit - tail[0:1]) * scale
                weight = jnp.where(point >= 0, weight, 0.0)
                lifted[i * unroll + u] = (mine[0:channels] * weight).astype(BF)
        leave(i).start()
        return carry

    def leave(i):
        at = pl.ds(i * unroll, unroll)
        return pltpu.make_async_copy(lifted.at[at], out.at[at], sems.at[3 + i])

    lax.fori_loop(0, send.shape[0] // unroll, step, 0)
    for i in range(send.shape[0] // unroll):
        leave(i).wait()


def lift(context, logits, send):
    channels, pixels = context.shape
    return pl.pallas_call(
        functools.partial(lift_kernel, 32),
        out_shape=jax.ShapeDtypeStruct((send.shape[0], channels, send.shape[1]), BF),
        in_specs=[pl.BlockSpec(memory_space=pl.ANY)] * 3,
        out_specs=pl.BlockSpec(memory_space=pl.ANY),
        scratch_shapes=[
            pltpu.VMEM((send.shape[0], channels, send.shape[1]), BF),
            pltpu.VMEM(context.shape, BF),
            pltpu.VMEM(logits.shape, BF),
            pltpu.VMEM(send.shape, jnp.int32),
            pltpu.VMEM((128, pixels), F32),
            pltpu.VMEM((channels + 128, pixels), BF),
            pltpu.SemaphoreType.DMA((3 + send.shape[0] // 32,)),
        ],
        compiler_params=params(60),
    )(context, logits, send)


def field_edges(field, tops, bottoms):
    tops[...] = field[:, 0:256]
    bottoms[...] = field[:, 2 * CELLS - 256 : 2 * CELLS]


def field_place(cell):
    row, x = (cell >> 6) & (SIDE - 1), cell & (SIDE - 1)
    return jnp.where(cell < 0, -1, row * 128 + (cell >> 12) * SIDE + x)


def list_starts(cells):
    half = (cells >> 10) & 3
    counts = jnp.stack([jnp.sum((cells >= 0) & (half == n), axis=1, dtype=jnp.int32) for n in range(LISTS)])
    return jnp.pad(jnp.cumsum(counts, axis=1), ((0, 0), (1, 0)))


def start_of(starts, n, s):
    first, last = starts[n, s], starts[n, s + 1]
    return first >> 7, first & 127, (last >> 7) > (first >> 7)


def plan_kernel(unroll, cells, starts, index, places, ranks, current):
    sources, slots = cells.shape
    below = lax.broadcasted_iota(jnp.int32, (slots, slots), 0)
    after = lax.broadcasted_iota(jnp.int32, (slots, slots), 1)
    earlier = jnp.where(below < after, 1.0, 0.0).astype(BF)
    cell = cells[...]
    for n in range(LISTS):
        member = jnp.where((cell >= 0) & (((cell >> 10) & 3) == n), 1.0, 0.0).astype(BF)
        found = jnp.dot(member, earlier, preferred_element_type=F32)
        ranks[n] = jnp.where(member.astype(F32) > 0.5, found, -1.0).astype(jnp.int32)
        places[n] = jnp.full(places.shape[1:], -1, jnp.int32)
    current[...] = jnp.full(current.shape, -1, jnp.int32)
    slot_iota = float_iota((slots, slots), 0)
    which = lax.broadcasted_iota(jnp.int32, (16, slots), 0)
    lane = lax.broadcasted_iota(jnp.int32, (1, slots), 1)
    one, zero = jnp.ones((), BF), jnp.zeros((), BF)

    def step(i, carry):
        for u in range(unroll):
            s = i * unroll + u
            place = field_place(cells[pl.ds(s, 1), :]) + 1
            rows = jnp.where(which == 0, lane, jnp.where(which == 1, place >> 6, place & 63))
            picks = []
            for n in range(LISTS):
                rank = ranks[n, pl.ds(s, 1), :]
                _, offset, _ = start_of(starts, n, s)
                to = jnp.where(rank < 0, -1, (rank + offset) & 127).astype(F32).astype(BF)
                picks.append(jnp.where(slot_iota == to, one, zero))
            found = lax.dot_general(
                rows.astype(F32).astype(BF),
                jnp.concatenate(picks, axis=0),
                (((1,), (1,)), ((), ())),
                preferred_element_type=F32,
            ).astype(jnp.int32)
            for n in range(LISTS):
                mine = found[:, n * slots : (n + 1) * slots]
                block, offset, full = start_of(starts, n, s)
                index[n, pl.ds(s, 1), :] = mine[0:1]
                place = mine[1:2] * 64 + mine[2:3] - 1
                stored = jnp.where(lane >= offset, place, current[n : n + 1, :])
                places[n, pl.ds(block, 1), :] = stored
                current[n : n + 1, :] = jnp.where(full, place, stored)
        return carry

    lax.fori_loop(0, sources // unroll, step, 0)
    for n in range(LISTS):
        total = starts[n, sources]
        places[n, pl.ds(total >> 7, 1), :] = jnp.where(lane < (total & 127), current[n : n + 1, :], -1)


LIST_BLOCK = 18


def plan(cells, starts):
    sources, slots = cells.shape
    blocks = sources + 2 * LIST_BLOCK
    return pl.pallas_call(
        functools.partial(plan_kernel, 16),
        out_shape=(
            jax.ShapeDtypeStruct((LISTS, sources, slots), jnp.int32),
            jax.ShapeDtypeStruct((LISTS, blocks, slots), jnp.int32),
        ),
        in_specs=[VMEM, SMEM],
        out_specs=(VMEM, VMEM),
        scratch_shapes=[pltpu.VMEM((LISTS, sources, slots), jnp.int32), pltpu.VMEM((8, slots), jnp.int32)],
        compiler_params=params(16),
        cost_estimate=pl.CostEstimate(flops=10**9, bytes_accessed=10**6, transcendentals=0),
    )(cells, starts)


def splat_kernel(
    groups, unroll, arrived, index, places, starts, bev, tops, bottoms, lists, total
):
    sources, channels, slots = arrived.shape
    width = total.shape[2]
    shift = width.bit_length() - 1
    lane = lax.broadcasted_iota(jnp.int32, (channels, slots), 1)
    nothing = jnp.zeros((channels, slots), F32)

    def put(n, block, value):
        lists[n, :, pl.ds(pl.multiple_of(block * slots, slots), slots)] = value.astype(BF)

    def gather(i, carry):
        carry = list(carry)
        for u in range(unroll):
            s = i * unroll + u
            values = arrived[s].astype(F32)
            for n in range(LISTS):
                block, offset, full = start_of(starts, n, s)
                source = jnp.broadcast_to(index[n, pl.ds(s, 1), :], values.shape)
                moved = jnp.take_along_axis(values, source, axis=1, mode="promise_in_bounds")
                stored = jnp.where(lane >= offset, moved, carry[n])
                put(n, block, stored)
                carry[n] = jnp.where(full, moved, stored)
        return tuple(carry)

    rest = lax.fori_loop(0, sources // unroll, gather, (nothing,) * LISTS)
    for n in range(LISTS):
        end = starts[n, sources] >> 7
        put(n, end, rest[n])
        for b in range(1, LIST_BLOCK + 1):
            put(n, end + b, nothing)
    total[...] = jnp.zeros(total.shape, F32)
    span = slots * LIST_BLOCK
    block = 256
    cell_iota = float_iota((block, span), 0)
    one, zero = jnp.ones((), BF), jnp.zeros((), BF)
    for n in range(LISTS):

        def step(i, carry):
            values = lists[n, :, pl.ds(pl.multiple_of(i * span, span), span)]
            rows = [places[n, pl.ds(i * LIST_BLOCK + u, 1), :] for u in range(LIST_BLOCK)]
            target = jnp.concatenate(rows, axis=1)
            target = jnp.where(target < 0, -1, target - n * (2 * CELLS // LISTS))
            group = target >> shift
            place = target & (width - 1)
            masked = [values * jnp.where(group == g, 1.0, 0.0).astype(BF) for g in range(groups)]
            grouped = jnp.concatenate(masked, axis=0)
            for j in range(width // block):
                spot = (place - j * block).astype(F32).astype(BF)
                pick = jnp.where(cell_iota == spot, one, zero)
                total[n, :, j * block : (j + 1) * block] += lax.dot_general(
                    grouped, pick, (((1,), (1,)), ((), ())), preferred_element_type=F32
                )
            return carry

        lax.fori_loop(0, (starts[n, sources] + span - 1) // span, step, 0)
        for g in range(groups):
            at = slice((n * groups + g) * width, (n * groups + g + 1) * width)
            bev[:, at] = total[n, g * channels : (g + 1) * channels, :].astype(BF)
    field_edges(bev, tops, bottoms)


def splat(arrived, index, places, starts):
    sources, channels, slots = arrived.shape
    groups = 4
    edge = jax.ShapeDtypeStruct((channels, 256), BF)
    return pl.pallas_call(
        functools.partial(splat_kernel, groups, 16),
        out_shape=(jax.ShapeDtypeStruct((channels, 2 * CELLS), BF), edge, edge),
        in_specs=[VMEM, VMEM, VMEM, SMEM],
        out_specs=(VMEM,) * 3,
        scratch_shapes=[
            pltpu.VMEM((LISTS, channels, (sources + 2 * LIST_BLOCK) * slots), BF),
            pltpu.VMEM((LISTS, groups * channels, 2 * CELLS // LISTS // groups), F32),
        ],
        compiler_params=params(32),
    )(arrived, index, places, starts)


def prepare_kernel(conv1, conv2, scale, bias, out_bias, weight1, weight2, vectors, square):
    channels, taps = scale.shape[1], weight1.shape[0]
    for source, target in ((conv1, weight1), (conv2, weight2)):
        for a in range(3):
            rows = source[:, a * taps : (a + 1) * taps]
            target[a * channels : (a + 1) * channels, :] = rows
    square[...] = jnp.zeros(square.shape, F32)
    for n, vector in enumerate((scale, bias, out_bias)):
        square[:, 0:channels] = jnp.broadcast_to(vector[...], (square.shape[0], channels))
        vectors[n] = jnp.transpose(square[...])[0:channels, :]


def prepare(conv1, conv2, scale, bias, out_bias):
    channels = conv1.shape[0]
    weight = jax.ShapeDtypeStruct((3 * channels, 3 * channels), BF)
    return pl.pallas_call(
        prepare_kernel,
        out_shape=(weight, weight, jax.ShapeDtypeStruct((3, channels, 128), F32)),
        in_specs=[VMEM] * 5,
        out_specs=(VMEM,) * 3,
        scratch_shapes=[pltpu.VMEM((128, 128), F32)],
        compiler_params=params(16),
        cost_estimate=pl.CostEstimate(flops=10**8, bytes_accessed=10**6, transcendentals=0),
    )(conv1, conv2, scale[None], bias[None], out_bias[None])


def conv_kernel(
    field,
    above,
    below,
    links,
    weight1,
    weight2,
    vectors,
    out,
    stack1,
    stack2,
    side_stack,
    result,
    sems,
):
    channels = field.shape[0]
    shape = (channels, 128)
    lane = lax.broadcasted_iota(jnp.int32, shape, 1)
    lower = lane < SIDE
    column = lane & (SIDE - 1)

    def gate(tile, n, want):
        return jnp.where(links[tile, n] == want, 1.0, 0.0)

    def block(ref, y):
        return ref[:, y * 128 : (y + 1) * 128]

    def put(stack, slot, left, center, right):
        for b, image in enumerate((left, center, right)):
            stack[b * channels : (b + 1) * channels, slot * 128 : (slot + 1) * 128] = image.astype(BF)

    def keeps(joined):
        left = jnp.where(lane == 0, 0.0, jnp.where(lane == SIDE, joined, 1.0))
        right = jnp.where(lane == 127, 0.0, jnp.where(lane == SIDE - 1, joined, 1.0))
        return left, right

    def put_row(stack, slot, row, keep):
        wide = row.astype(F32)
        put(stack, slot, pltpu.roll(wide, 1, 1) * keep[0], row, pltpu.roll(wide, 127, 1) * keep[1])

    def put_mapped(stack, slot, source, west, center, east, inverse=False):
        swapped = pltpu.roll(source, SIDE, 1)

        def mapped(n):
            cross = [gate(0, n, 1), gate(1, n, 0)]
            if inverse:
                cross.reverse()
            same = jnp.where(lower, gate(0, n, 0), gate(1, n, 1))
            return source * same + swapped * jnp.where(lower, cross[0], cross[1])

        middle = mapped(center)
        left = jnp.where(column == 0, pltpu.roll(mapped(west), SIDE + 1, 1), pltpu.roll(middle, 1, 1))
        right = jnp.where(
            column == SIDE - 1, pltpu.roll(mapped(east), SIDE - 1, 1), pltpu.roll(middle, 127, 1)
        )
        put(stack, slot, left, middle, right)

    def multiply(weight, stack, product, start, stop):
        found = jnp.dot(
            weight[...], stack[:, start * 128 : stop * 128], preferred_element_type=F32
        )
        for slot in range(start, stop):
            lanes = slice((slot - start) * 128, (slot - start + 1) * 128)
            for a in range(3):
                product[a, slot] = found[a * channels : (a + 1) * channels, lanes]

    def summed(product, slots):
        first, second, third = (product.pop((a, slot)) for a, slot in enumerate(slots))
        return first + second + third

    def joined(west, center, east):
        found = 0.0
        for j in range(2):
            for a, b in ((west, center), (center, east)):
                found = jnp.maximum(found, gate(j, a, 0) * gate(j, b, 1))
        return found

    gain, shift, last_shift = (vectors[n] for n in range(3))
    keep = keeps(gate(1, 3, 0))
    keep_up, keep_down = keeps(joined(0, 1, 2)), keeps(joined(5, 6, 7))
    end = SIDE + 1
    product1, product2, side_product = {}, {}, {}

    def activate(value):
        return jnp.maximum(gain * value + shift, 0.0).astype(BF)

    put_row(side_stack, 0, block(above, 0), keep_up)
    put_row(side_stack, 1, block(above, 1), keep_up)
    put_mapped(side_stack, 2, block(field, 0).astype(F32), 2, 1, 0, True)
    put_mapped(side_stack, 3, block(field, SIDE - 1).astype(F32), 7, 6, 5, True)
    put_row(side_stack, 4, block(below, 0), keep_down)
    put_row(side_stack, 5, block(below, 1), keep_down)
    multiply(weight1, side_stack, side_product, 0, 6)
    up_row = activate(summed(side_product, (0, 1, 2))).astype(F32)
    down_row = activate(summed(side_product, (3, 4, 5))).astype(F32)
    put_mapped(stack2, 0, up_row, 0, 1, 2)
    put_mapped(stack2, end, down_row, 5, 6, 7)
    put_mapped(stack1, 0, block(above, 1).astype(F32), 0, 1, 2)
    put_mapped(stack1, end, block(below, 0).astype(F32), 5, 6, 7)

    step = 16
    done = 0
    for start in range(0, SIDE + 2, step):
        stop = min(start + step, SIDE + 2)
        for slot in range(max(start, 1), min(stop, end)):
            put_row(stack1, slot, block(field, slot - 1), keep)
        multiply(weight1, stack1, product1, start, stop)
        while done < stop - 2:
            put_row(stack2, done + 1, activate(summed(product1, (done, done + 1, done + 2))), keep)
            done += 1

    copies = []
    done = 0
    part = 16
    for start in range(0, SIDE + 2, step):
        stop = min(start + step, SIDE + 2)
        multiply(weight2, stack2, product2, start, stop)
        while done + 1 < stop - 2:
            even = summed(product2, (done, done + 1, done + 2)) + last_shift
            odd = summed(product2, (done + 1, done + 2, done + 3)) + last_shift
            at = slice(done * SIDE, (done + 2) * SIDE)
            result[0, :, at] = jnp.where(lower, even, pltpu.roll(odd, SIDE, 1))
            result[1, :, at] = jnp.where(lower, pltpu.roll(even, SIDE, 1), odd)
            done += 2
            if done % part == 0:
                n = done // part - 1
                at = slice(n * part * SIDE, (n + 1) * part * SIDE)
                for tile in range(2):
                    copy = pltpu.make_async_copy(
                        result.at[tile, :, at], out.at[tile, :, at], sems.at[tile, n]
                    )
                    copy.start()
                    copies.append(copy)
    for copy in copies:
        copy.wait()


def convolutions(field, above, below, links, weight1, weight2, vectors):
    channels = field.shape[0]
    stack = pltpu.VMEM((3 * channels, (SIDE + 2) * 128), BF)
    return pl.pallas_call(
        conv_kernel,
        out_shape=jax.ShapeDtypeStruct((2, channels, CELLS), F32),
        in_specs=[VMEM, VMEM, VMEM, SMEM] + [VMEM] * 3,
        out_specs=pl.BlockSpec(memory_space=pl.ANY),
        scratch_shapes=[
            stack,
            stack,
            pltpu.VMEM((3 * channels, 768), BF),
            pltpu.VMEM((2, channels, CELLS), F32),
            pltpu.SemaphoreType.DMA((2, 4)),
        ],
        compiler_params=params(44),
    )(field, above, below, links, weight1, weight2, vectors)


def exchange(tops, bottoms):
    devices = lax.axis_size("dev")
    above = lax.ppermute(bottoms, "dev", [(i, i + 1) for i in range(devices - 1)])
    below = lax.ppermute(tops, "dev", [(i + 1, i) for i in range(devices - 1)])
    return above, below


def per_device(
    context,
    depth_logits,
    send_point,
    recv_cell,
    neighbour,
    conv1_weight,
    layer_scale,
    layer_bias,
    conv2_weight,
    out_bias,
):
    lifted = lift(context, depth_logits, send_point[0])
    arrived = lax.all_to_all(lifted, "dev", split_axis=0, concat_axis=0, tiled=True)
    starts = list_starts(recv_cell[0])
    index, places = plan(recv_cell[0], starts)
    prepared = prepare(conv1_weight, conv2_weight, layer_scale, layer_bias, out_bias)
    places, prepared = lax.optimization_barrier((places, prepared))
    bev, tops, bottoms = splat(arrived, index, places, starts)
    above, below = exchange(tops, bottoms)
    out = convolutions(bev, above, below, neighbour[0], *prepared)
    return out[None]


def solution(mesh):
    in_specs = (
        P(None, "dev"),
        P(None, "dev"),
        P("dev", None, None),
        P("dev", None, None),
        P("dev", None, None),
        P(),
        P(),
        P(),
        P(),
        P(),
    )
    out_specs = P("dev", None, None, None)
    return jax.shard_map(
        per_device, mesh=mesh, in_specs=in_specs, out_specs=out_specs, check_vma=False
    )
```

```python
import functools

import jax
import jax.numpy as jnp
from jax import lax
from jax.experimental import pallas as pl
from jax.experimental.pallas import tpu as pltpu
from jax.sharding import PartitionSpec as P

SIDE = 64
CELLS = SIDE * SIDE
LISTS = 4
BF = jnp.bfloat16
F32 = jnp.float32
VMEM = pl.BlockSpec(memory_space=pltpu.VMEM)
SMEM = pl.BlockSpec(memory_space=pltpu.SMEM)


def params(megabytes):
    return pltpu.CompilerParams(vmem_limit_bytes=megabytes * 1024 * 1024)


def float_iota(shape, axis):
    return lax.broadcasted_iota(jnp.int32, shape, axis).astype(F32).astype(BF)


def split_high(value):
    high = value.astype(BF).astype(F32)
    return high, value - high


def lift_kernel(unroll, context_in, logits_in, send_in, out, lifted, context, logits, send, wide, table, sems):
    pairs = ((logits_in, logits), (context_in, context), (send_in, send))
    copies = [pltpu.make_async_copy(a, b, sems.at[n]) for n, (a, b) in enumerate(pairs)]
    for copy in copies:
        copy.start()
    channels, pixels = context.shape
    depths = logits.shape[0]
    slots = send.shape[1]
    bins = -(-depths // 8) * 8
    copies[0].wait()
    values = logits[...].astype(F32)
    largest = jnp.max(values, axis=0, keepdims=True)
    inverse = 1.0 / jnp.sum(jnp.exp(values - largest), axis=0, keepdims=True)
    wide[...] = jnp.zeros(wide.shape, F32)
    wide[0:depths, :] = values
    wide[bins : bins + 1, :] = largest
    for n in range(3):
        high, inverse = split_high(inverse)
        wide[bins + 1 + n : bins + 2 + n, :] = high
    copies[1].wait()
    copies[2].wait()
    table[0:channels, :] = context[...]
    table[channels:, :] = wide[...].astype(BF)
    pixel_iota = float_iota((pixels, slots), 0)
    bin_iota = lax.broadcasted_iota(jnp.int32, (8, slots), 0)
    one, zero = jnp.ones((), BF), jnp.zeros((), BF)

    def step(i, carry):
        points = [send[pl.ds(i * unroll + u, 1), :] for u in range(unroll)]
        picks = []
        for point in points:
            pixel = (point & (pixels - 1)).astype(F32).astype(BF)
            picks.append(jnp.where(pixel_iota == pixel, one, zero))
        for v in range(0, unroll, 2):
            found = jnp.dot(
                table[...], jnp.concatenate(picks[v : v + 2], axis=1), preferred_element_type=F32
            )
            for u in (v, v + 1):
                point = points[u]
                mine = found[:, (u - v) * slots : (u - v + 1) * slots]
                offset = (point >> 8) - bin_iota
                chosen = jnp.zeros((8, slots), F32)
                for r in range(0, bins, 8):
                    chosen = jnp.where(offset == r, mine[channels + r : channels + r + 8], chosen)
                logit = jnp.sum(chosen, axis=0, keepdims=True)
                tail = mine[channels + bins :]
                scale = tail[1:2] + tail[2:3] + tail[3:4]
                weight = jnp.exp(logit - tail[0:1]) * scale
                weight = jnp.where(point >= 0, weight, 0.0)
                lifted[i * unroll + u] = (mine[0:channels] * weight).astype(BF)
        leave(i).start()
        return carry

    def leave(i):
        at = pl.ds(i * unroll, unroll)
        return pltpu.make_async_copy(lifted.at[at], out.at[at], sems.at[3 + i])

    lax.fori_loop(0, send.shape[0] // unroll, step, 0)
    for i in range(send.shape[0] // unroll):
        leave(i).wait()


def lift(context, logits, send):
    channels, pixels = context.shape
    return pl.pallas_call(
        functools.partial(lift_kernel, 32),
        out_shape=jax.ShapeDtypeStruct((send.shape[0], channels, send.shape[1]), BF),
        in_specs=[pl.BlockSpec(memory_space=pl.ANY)] * 3,
        out_specs=pl.BlockSpec(memory_space=pl.ANY),
        scratch_shapes=[
            pltpu.VMEM((send.shape[0], channels, send.shape[1]), BF),
            pltpu.VMEM(context.shape, BF),
            pltpu.VMEM(logits.shape, BF),
            pltpu.VMEM(send.shape, jnp.int32),
            pltpu.VMEM((128, pixels), F32),
            pltpu.VMEM((channels + 128, pixels), BF),
            pltpu.SemaphoreType.DMA((3 + send.shape[0] // 32,)),
        ],
        compiler_params=params(60),
    )(context, logits, send)


def field_edges(field, tops, bottoms):
    tops[...] = field[:, 0:256]
    bottoms[...] = field[:, 2 * CELLS - 256 : 2 * CELLS]


def field_place(cell):
    row, x = (cell >> 6) & (SIDE - 1), cell & (SIDE - 1)
    return jnp.where(cell < 0, -1, row * 128 + (cell >> 12) * SIDE + x)


def list_starts(cells):
    half = (cells >> 10) & 3
    counts = jnp.stack([jnp.sum((cells >= 0) & (half == n), axis=1, dtype=jnp.int32) for n in range(LISTS)])
    return jnp.pad(jnp.cumsum(counts, axis=1), ((0, 0), (1, 0)))


def start_of(starts, n, s):
    first, last = starts[n, s], starts[n, s + 1]
    return first >> 7, first & 127, (last >> 7) > (first >> 7)


def plan_kernel(unroll, cells, starts, index, places, ranks, current):
    sources, slots = cells.shape
    below = lax.broadcasted_iota(jnp.int32, (slots, slots), 0)
    after = lax.broadcasted_iota(jnp.int32, (slots, slots), 1)
    earlier = jnp.where(below < after, 1.0, 0.0).astype(BF)
    cell = cells[...]
    for n in range(LISTS):
        member = jnp.where((cell >= 0) & (((cell >> 10) & 3) == n), 1.0, 0.0).astype(BF)
        found = jnp.dot(member, earlier, preferred_element_type=F32)
        ranks[n] = jnp.where(member.astype(F32) > 0.5, found, -1.0).astype(jnp.int32)
        places[n] = jnp.full(places.shape[1:], -1, jnp.int32)
    current[...] = jnp.full(current.shape, -1, jnp.int32)
    slot_iota = float_iota((slots, slots), 0)
    which = lax.broadcasted_iota(jnp.int32, (16, slots), 0)
    lane = lax.broadcasted_iota(jnp.int32, (1, slots), 1)
    one, zero = jnp.ones((), BF), jnp.zeros((), BF)

    def step(i, carry):
        for u in range(unroll):
            s = i * unroll + u
            place = field_place(cells[pl.ds(s, 1), :]) + 1
            rows = jnp.where(which == 0, lane, jnp.where(which == 1, place >> 6, place & 63))
            picks = []
            for n in range(LISTS):
                rank = ranks[n, pl.ds(s, 1), :]
                _, offset, _ = start_of(starts, n, s)
                to = jnp.where(rank < 0, -1, (rank + offset) & 127).astype(F32).astype(BF)
                picks.append(jnp.where(slot_iota == to, one, zero))
            found = lax.dot_general(
                rows.astype(F32).astype(BF),
                jnp.concatenate(picks, axis=0),
                (((1,), (1,)), ((), ())),
                preferred_element_type=F32,
            ).astype(jnp.int32)
            for n in range(LISTS):
                mine = found[:, n * slots : (n + 1) * slots]
                block, offset, full = start_of(starts, n, s)
                index[n, pl.ds(s, 1), :] = mine[0:1]
                place = mine[1:2] * 64 + mine[2:3] - 1
                stored = jnp.where(lane >= offset, place, current[n : n + 1, :])
                places[n, pl.ds(block, 1), :] = stored
                current[n : n + 1, :] = jnp.where(full, place, stored)
        return carry

    lax.fori_loop(0, sources // unroll, step, 0)
    for n in range(LISTS):
        total = starts[n, sources]
        places[n, pl.ds(total >> 7, 1), :] = jnp.where(lane < (total & 127), current[n : n + 1, :], -1)


LIST_BLOCK = 34


def plan(cells, starts):
    sources, slots = cells.shape
    blocks = sources + LIST_BLOCK + 6
    return pl.pallas_call(
        functools.partial(plan_kernel, 16),
        out_shape=(
            jax.ShapeDtypeStruct((LISTS, sources, slots), jnp.int32),
            jax.ShapeDtypeStruct((LISTS, blocks, slots), jnp.int32),
        ),
        in_specs=[VMEM, SMEM],
        out_specs=(VMEM, VMEM),
        scratch_shapes=[pltpu.VMEM((LISTS, sources, slots), jnp.int32), pltpu.VMEM((8, slots), jnp.int32)],
        compiler_params=params(16),
        cost_estimate=pl.CostEstimate(flops=10**9, bytes_accessed=10**6, transcendentals=0),
    )(cells, starts)


def splat_kernel(
    groups, unroll, arrived, index, places, starts, bev, tops, bottoms, lists, total
):
    sources, channels, slots = arrived.shape
    width = total.shape[2]
    shift = width.bit_length() - 1
    lane = lax.broadcasted_iota(jnp.int32, (channels, slots), 1)
    nothing = jnp.zeros((channels, slots), F32)

    def put(n, block, value):
        lists[n, :, pl.ds(pl.multiple_of(block * slots, slots), slots)] = value.astype(BF)

    def gather(i, carry):
        carry = list(carry)
        for u in range(unroll):
            s = i * unroll + u
            values = arrived[s].astype(F32)
            for n in range(LISTS):
                block, offset, full = start_of(starts, n, s)
                source = jnp.broadcast_to(index[n, pl.ds(s, 1), :], values.shape)
                moved = jnp.take_along_axis(values, source, axis=1, mode="promise_in_bounds")
                stored = jnp.where(lane >= offset, moved, carry[n])
                put(n, block, stored)
                carry[n] = jnp.where(full, moved, stored)
        return tuple(carry)

    rest = lax.fori_loop(0, sources // unroll, gather, (nothing,) * LISTS)
    for n in range(LISTS):
        end = starts[n, sources] >> 7
        put(n, end, rest[n])
        for b in range(1, LIST_BLOCK + 1):
            put(n, end + b, nothing)
    total[...] = jnp.zeros(total.shape, F32)
    span = slots * LIST_BLOCK
    block = 256
    cell_iota = float_iota((block, span), 0)
    one, zero = jnp.ones((), BF), jnp.zeros((), BF)
    for n in range(LISTS):

        def step(i, carry):
            values = lists[n, :, pl.ds(pl.multiple_of(i * span, span), span)]
            rows = [places[n, pl.ds(i * LIST_BLOCK + u, 1), :] for u in range(LIST_BLOCK)]
            target = jnp.concatenate(rows, axis=1)
            target = jnp.where(target < 0, -1, target - n * (2 * CELLS // LISTS))
            group = target >> shift
            place = target & (width - 1)
            masked = [values * jnp.where(group == g, 1.0, 0.0).astype(BF) for g in range(groups)]
            grouped = jnp.concatenate(masked, axis=0)
            for j in range(width // block):
                spot = (place - j * block).astype(F32).astype(BF)
                pick = jnp.where(cell_iota == spot, one, zero)
                total[n, :, j * block : (j + 1) * block] += lax.dot_general(
                    grouped, pick, (((1,), (1,)), ((), ())), preferred_element_type=F32
                )
            return carry

        lax.fori_loop(0, (starts[n, sources] + span - 1) // span, step, 0)
        for g in range(groups):
            at = slice((n * groups + g) * width, (n * groups + g + 1) * width)
            bev[:, at] = total[n, g * channels : (g + 1) * channels, :].astype(BF)
    field_edges(bev, tops, bottoms)


def splat(arrived, index, places, starts):
    sources, channels, slots = arrived.shape
    groups = 4
    edge = jax.ShapeDtypeStruct((channels, 256), BF)
    return pl.pallas_call(
        functools.partial(splat_kernel, groups, 32),
        out_shape=(jax.ShapeDtypeStruct((channels, 2 * CELLS), BF), edge, edge),
        in_specs=[VMEM, VMEM, VMEM, SMEM],
        out_specs=(VMEM,) * 3,
        scratch_shapes=[
            pltpu.VMEM((LISTS, channels, (sources + LIST_BLOCK + 6) * slots), BF),
            pltpu.VMEM((LISTS, groups * channels, 2 * CELLS // LISTS // groups), F32),
        ],
        compiler_params=params(32),
    )(arrived, index, places, starts)


def prepare_kernel(conv1, conv2, scale, bias, out_bias, weight1, weight2, vectors, square):
    channels, taps = scale.shape[1], weight1.shape[0]
    for source, target in ((conv1, weight1), (conv2, weight2)):
        for a in range(3):
            rows = source[:, a * taps : (a + 1) * taps]
            target[a * channels : (a + 1) * channels, :] = rows
    square[...] = jnp.zeros(square.shape, F32)
    for n, vector in enumerate((scale, bias, out_bias)):
        square[:, 0:channels] = jnp.broadcast_to(vector[...], (square.shape[0], channels))
        vectors[n] = jnp.transpose(square[...])[0:channels, :]


def prepare(conv1, conv2, scale, bias, out_bias):
    channels = conv1.shape[0]
    weight = jax.ShapeDtypeStruct((3 * channels, 3 * channels), BF)
    return pl.pallas_call(
        prepare_kernel,
        out_shape=(weight, weight, jax.ShapeDtypeStruct((3, channels, 128), F32)),
        in_specs=[VMEM] * 5,
        out_specs=(VMEM,) * 3,
        scratch_shapes=[pltpu.VMEM((128, 128), F32)],
        compiler_params=params(16),
        cost_estimate=pl.CostEstimate(flops=10**8, bytes_accessed=10**6, transcendentals=0),
    )(conv1, conv2, scale[None], bias[None], out_bias[None])


def conv_kernel(
    field,
    above,
    below,
    links,
    weight1,
    weight2,
    vectors,
    out,
    stack1,
    stack2,
    side_stack,
    result,
    sems,
):
    channels = field.shape[0]
    shape = (channels, 128)
    lane = lax.broadcasted_iota(jnp.int32, shape, 1)
    lower = lane < SIDE
    column = lane & (SIDE - 1)

    def gate(tile, n, want):
        return jnp.where(links[tile, n] == want, 1.0, 0.0)

    def block(ref, y):
        return ref[:, y * 128 : (y + 1) * 128]

    def put(stack, slot, left, center, right):
        for b, image in enumerate((left, center, right)):
            stack[b * channels : (b + 1) * channels, slot * 128 : (slot + 1) * 128] = image.astype(BF)

    def keeps(joined):
        left = jnp.where(lane == 0, 0.0, jnp.where(lane == SIDE, joined, 1.0))
        right = jnp.where(lane == 127, 0.0, jnp.where(lane == SIDE - 1, joined, 1.0))
        return left, right

    def put_row(stack, slot, row, keep):
        wide = row.astype(F32)
        put(stack, slot, pltpu.roll(wide, 1, 1) * keep[0], row, pltpu.roll(wide, 127, 1) * keep[1])

    def put_mapped(stack, slot, source, west, center, east, inverse=False):
        swapped = pltpu.roll(source, SIDE, 1)

        def mapped(n):
            cross = [gate(0, n, 1), gate(1, n, 0)]
            if inverse:
                cross.reverse()
            same = jnp.where(lower, gate(0, n, 0), gate(1, n, 1))
            return source * same + swapped * jnp.where(lower, cross[0], cross[1])

        middle = mapped(center)
        left = jnp.where(column == 0, pltpu.roll(mapped(west), SIDE + 1, 1), pltpu.roll(middle, 1, 1))
        right = jnp.where(
            column == SIDE - 1, pltpu.roll(mapped(east), SIDE - 1, 1), pltpu.roll(middle, 127, 1)
        )
        put(stack, slot, left, middle, right)

    def multiply(weight, stack, product, start, stop):
        found = jnp.dot(
            weight[...], stack[:, start * 128 : stop * 128], preferred_element_type=F32
        )
        for slot in range(start, stop):
            lanes = slice((slot - start) * 128, (slot - start + 1) * 128)
            for a in range(3):
                product[a, slot] = found[a * channels : (a + 1) * channels, lanes]

    def summed(product, slots):
        first, second, third = (product.pop((a, slot)) for a, slot in enumerate(slots))
        return first + second + third

    def joined(west, center, east):
        found = 0.0
        for j in range(2):
            for a, b in ((west, center), (center, east)):
                found = jnp.maximum(found, gate(j, a, 0) * gate(j, b, 1))
        return found

    gain, shift, last_shift = (vectors[n] for n in range(3))
    keep = keeps(gate(1, 3, 0))
    keep_up, keep_down = keeps(joined(0, 1, 2)), keeps(joined(5, 6, 7))
    end = SIDE + 1
    product1, product2, side_product = {}, {}, {}

    def activate(value):
        return jnp.maximum(gain * value + shift, 0.0).astype(BF)

    put_row(side_stack, 0, block(above, 0), keep_up)
    put_row(side_stack, 1, block(above, 1), keep_up)
    put_mapped(side_stack, 2, block(field, 0).astype(F32), 2, 1, 0, True)
    put_mapped(side_stack, 3, block(field, SIDE - 1).astype(F32), 7, 6, 5, True)
    put_row(side_stack, 4, block(below, 0), keep_down)
    put_row(side_stack, 5, block(below, 1), keep_down)
    multiply(weight1, side_stack, side_product, 0, 6)
    up_row = activate(summed(side_product, (0, 1, 2))).astype(F32)
    down_row = activate(summed(side_product, (3, 4, 5))).astype(F32)
    put_mapped(stack2, 0, up_row, 0, 1, 2)
    put_mapped(stack2, end, down_row, 5, 6, 7)
    put_mapped(stack1, 0, block(above, 1).astype(F32), 0, 1, 2)
    put_mapped(stack1, end, block(below, 0).astype(F32), 5, 6, 7)

    step = 16
    done = 0
    for start in range(0, SIDE + 2, step):
        stop = min(start + step, SIDE + 2)
        for slot in range(max(start, 1), min(stop, end)):
            put_row(stack1, slot, block(field, slot - 1), keep)
        multiply(weight1, stack1, product1, start, stop)
        while done < stop - 2:
            put_row(stack2, done + 1, activate(summed(product1, (done, done + 1, done + 2))), keep)
            done += 1

    copies = []
    done = 0
    part = 16
    for start in range(0, SIDE + 2, step):
        stop = min(start + step, SIDE + 2)
        multiply(weight2, stack2, product2, start, stop)
        while done + 1 < stop - 2:
            even = summed(product2, (done, done + 1, done + 2)) + last_shift
            odd = summed(product2, (done + 1, done + 2, done + 3)) + last_shift
            at = slice(done * SIDE, (done + 2) * SIDE)
            result[0, :, at] = jnp.where(lower, even, pltpu.roll(odd, SIDE, 1))
            result[1, :, at] = jnp.where(lower, pltpu.roll(even, SIDE, 1), odd)
            done += 2
            if done % part == 0:
                n = done // part - 1
                at = slice(n * part * SIDE, (n + 1) * part * SIDE)
                for tile in range(2):
                    copy = pltpu.make_async_copy(
                        result.at[tile, :, at], out.at[tile, :, at], sems.at[tile, n]
                    )
                    copy.start()
                    copies.append(copy)
    for copy in copies:
        copy.wait()


def convolutions(field, above, below, links, weight1, weight2, vectors):
    channels = field.shape[0]
    stack = pltpu.VMEM((3 * channels, (SIDE + 2) * 128), BF)
    return pl.pallas_call(
        conv_kernel,
        out_shape=jax.ShapeDtypeStruct((2, channels, CELLS), F32),
        in_specs=[VMEM, VMEM, VMEM, SMEM] + [VMEM] * 3,
        out_specs=pl.BlockSpec(memory_space=pl.ANY),
        scratch_shapes=[
            stack,
            stack,
            pltpu.VMEM((3 * channels, 768), BF),
            pltpu.VMEM((2, channels, CELLS), F32),
            pltpu.SemaphoreType.DMA((2, 4)),
        ],
        compiler_params=params(44),
    )(field, above, below, links, weight1, weight2, vectors)


def exchange(tops, bottoms):
    devices = lax.axis_size("dev")
    above = lax.ppermute(bottoms, "dev", [(i, i + 1) for i in range(devices - 1)])
    below = lax.ppermute(tops, "dev", [(i + 1, i) for i in range(devices - 1)])
    return above, below


def per_device(
    context,
    depth_logits,
    send_point,
    recv_cell,
    neighbour,
    conv1_weight,
    layer_scale,
    layer_bias,
    conv2_weight,
    out_bias,
):
    lifted = lift(context, depth_logits, send_point[0])
    arrived = lax.all_to_all(lifted, "dev", split_axis=0, concat_axis=0, tiled=True)
    starts = list_starts(recv_cell[0])
    index, places = plan(recv_cell[0], starts)
    prepared = prepare(conv1_weight, conv2_weight, layer_scale, layer_bias, out_bias)
    places, prepared = lax.optimization_barrier((places, prepared))
    bev, tops, bottoms = splat(arrived, index, places, starts)
    above, below = exchange(tops, bottoms)
    out = convolutions(bev, above, below, neighbour[0], *prepared)
    return out[None]


def solution(mesh):
    in_specs = (
        P(None, "dev"),
        P(None, "dev"),
        P("dev", None, None),
        P("dev", None, None),
        P("dev", None, None),
        P(),
        P(),
        P(),
        P(),
        P(),
    )
    out_specs = P("dev", None, None, None)
    return jax.shard_map(
        per_device, mesh=mesh, in_specs=in_specs, out_specs=out_specs, check_vma=False
    )
```
